128 devices in a mesh: space: 32 (over z, y, core), orb: 4 (over x).
Axes of the slice: x: 4, y: 4, z: 4, core: 2. Of those that a mesh axis runs over, the one named last changes fastest.
Arguments:
- orbitals: float32 [8, 32768, 256], P('orb', 'space'), may hold values from -6 to 6
- near_source: int32 [32768, 27], P('space'), may hold values from 0 to 32767, as said below
- far_leaf: int32 [32768, 108], P('space'), may hold values from 0 to 32767, as said below
- far_mid: int32 [4096, 108], P('space'), may hold values from 0 to 4095, as said below
- far_top: int32 [512, 108], P('space'), may hold values from 0 to 511, as said below
- leaf_basis: bfloat16 [64, 256], replicated, may hold values from -0.375 to 0.375
- near_table: bfloat16 [27, 256, 256], replicated, may hold values from -0.078125 to 0.078125
- transfer: bfloat16 [8, 64, 64], replicated, may hold values from -0.75 to 0.75
- coupling: bfloat16 [108, 64, 64], replicated, may hold values from -0.078125 to 0.078125
- pair_transfer: bfloat16 [2, 64, 64], replicated, may hold values from -0.75 to 0.75
- coarse_coupling: bfloat16 [4, 64, 64], replicated, may hold values from -0.4375 to 0.4375
Outputs:
- relaxed: float32 [8, 32768, 256], P('orb', 'space')
The draws below stay inside these ranges and needn't reach their ends.
Inputs may be any that keep to these rules, and one draw needn't show every extreme that they name: `near_source`: with layer(t) = t // 64: every entry of leaf t lies in a layer at most 1 from layer(t); entry 13 is t itself; entry 0 is the leaf at t's transverse position one layer away. `far_leaf`: with layer(t) = t // 64: every entry of box t lies in a layer 2 or 3 away from layer(t); entry 0 is exactly 3 layers away. `far_mid`: with layer(t) = t // 16: every entry of box t lies in a layer 2 or 3 away from layer(t); entry 0 is exactly 3 layers away. `far_top`: with layer(t) = t // 4: every entry of box t lies in a layer 2 or 3 away from layer(t); entry 0 is exactly 3 layers away.
All inputs are finite; a program needn't handle non-finite values.
Results may differ from the reference program's by a relative error of at most 0.012.
Values may be sent and summed in bfloat16 or wider, within the bound.
A program may use at most 192 MiB of HBM per device.

```python
import jax
import jax.numpy as jnp
from jax import lax

PTS = 256
RANK = 64
ORB = 8
KNEAR = 27
KFAR = 108
SIDE = 8
LEAVES = 32768
MIDS = 4096
TOPS = 512


def layered_list(key, box_count, layer_size, slot_count, nearby):
    first_key, second_key, third_key = jax.random.split(key, 3)
    target = jnp.arange(box_count, dtype=jnp.int32)
    layer_of = target // layer_size
    inside = target % layer_size
    layers = box_count // layer_size
    if nearby:
        layer_step = jax.random.randint(first_key, (box_count, slot_count), -1, 2, dtype=jnp.int32)
        chosen = jnp.clip(layer_of[:, None] + layer_step, 0, layers - 1)
        forced = jnp.where(layer_of + 1 < layers, layer_of + 1, layer_of - 1)
    else:
        sign_draw = jax.random.randint(first_key, (box_count, slot_count), 0, 2, dtype=jnp.int32) * 2 - 1
        distance = jax.random.randint(third_key, (box_count, slot_count), 2, 4, dtype=jnp.int32)
        chosen = layer_of[:, None] + sign_draw * distance
        outside = (chosen < 0) | (chosen >= layers)
        chosen = jnp.where(outside, layer_of[:, None] - sign_draw * distance, chosen)
        forced = jnp.where(layer_of + 3 < layers, layer_of + 3, layer_of - 3)
    positions = jax.random.randint(second_key, (box_count, slot_count), 0, layer_size, dtype=jnp.int32)
    sources = chosen * layer_size + positions
    sources = sources.at[:, 0].set(forced * layer_size + inside)
    if nearby:
        sources = sources.at[:, 13].set(target)
    return sources.astype(jnp.int32)


def draw_near_source(key, part):
    return layered_list(jax.random.fold_in(key, 11), LEAVES, SIDE * SIDE, KNEAR, True)


def draw_far_leaf(key, part):
    return layered_list(jax.random.fold_in(key, 23), LEAVES, SIDE * SIDE, KFAR, False)


def draw_far_mid(key, part):
    return layered_list(jax.random.fold_in(key, 37), MIDS, SIDE // 2 * (SIDE // 2), KFAR, False)


def draw_far_top(key, part):
    return layered_list(jax.random.fold_in(key, 41), TOPS, SIDE // 4 * (SIDE // 4), KFAR, False)


def block_scale(stream_key, extent, shards, low, largest):
    def one(axis_at, shards_of):
        steps = jax.random.uniform(jax.random.fold_in(jax.random.fold_in(stream_key, 6), axis_at), (shards_of,), jnp.float32, low / len(shards), largest / len(shards))
        return jnp.repeat(jnp.exp(steps), extent[axis_at] // shards_of).reshape((-1,) + (1,) * (len(extent) - axis_at - 1))

    loudness = one(*shards[0])
    for cut in shards[1:]:
        loudness = loudness * one(*cut)
    return loudness


def gaussian(stream_key, shape, width, most, cuts=(), kind=jnp.bfloat16):
    factor_of = block_scale(stream_key, shape, cuts, -0.22, 0.18) if cuts else 1.0
    array = jax.random.normal(stream_key, shape, jnp.float32) * width * factor_of
    return jnp.minimum(jnp.maximum(array, -most), most).astype(kind)


def setup_inputs(seed: int = 0) -> dict:
    streams_of = jax.random.split(jax.random.key(seed), 12)
    orbitals = gaussian(streams_of[0], (ORB, LEAVES, PTS), 1.0, 6.0, ((0, 4), (1, 32)), jnp.float32)
    near_source = draw_near_source(jax.random.fold_in(streams_of[11], 71), 0)
    far_leaf = draw_far_leaf(jax.random.fold_in(streams_of[11], 71), 0)
    far_mid = draw_far_mid(jax.random.fold_in(streams_of[11], 71), 0)
    far_top = draw_far_top(jax.random.fold_in(streams_of[11], 71), 0)
    leaf_basis = gaussian(streams_of[5], (RANK, PTS), PTS ** -0.5, 0.375)
    near_table = gaussian(streams_of[6], (KNEAR, PTS, PTS), (KNEAR * PTS) ** -0.5, 0.078125)
    transfer = gaussian(streams_of[7], (8, RANK, RANK), RANK ** -0.5, 0.75)
    coupling = gaussian(streams_of[8], (KFAR, RANK, RANK), (KFAR * RANK) ** -0.5, 0.078125)
    pair_transfer = gaussian(streams_of[9], (2, RANK, RANK), RANK ** -0.5, 0.75)
    coarse_coupling = gaussian(streams_of[10], (4, RANK, RANK), (3 * RANK) ** -0.5, 0.4375)
    return dict(orbitals=orbitals, near_source=near_source, far_leaf=far_leaf, far_mid=far_mid, far_top=far_top, leaf_basis=leaf_basis, near_table=near_table, transfer=transfer, coupling=coupling, pair_transfer=pair_transfer, coarse_coupling=coarse_coupling)


relax_step = 0.1


def octant_up(moments, side_boxes, transfer):
    orbits, node_count, rank_width = moments.shape
    layers = node_count // (side_boxes * side_boxes)
    half_side = side_boxes // 2
    shaped = moments.reshape(orbits, layers // 2, 2, half_side, 2, half_side, 2, rank_width).astype(jnp.float32)
    octant_grid = transfer.reshape(2, 2, 2, rank_width, rank_width).astype(jnp.float32)
    parents = jnp.einsum("oapbqcus,pqusr->oabcr", shaped, octant_grid)
    return parents.reshape(orbits, -1, rank_width).astype(jnp.bfloat16)


def octant_down(coeffs, side_boxes, transfer):
    orbits, node_count, rank_width = coeffs.shape
    layers = node_count // (side_boxes * side_boxes)
    shaped = coeffs.reshape(orbits, layers, side_boxes, side_boxes, rank_width).astype(jnp.float32)
    octant_grid = transfer.reshape(2, 2, 2, rank_width, rank_width).astype(jnp.float32)
    children = jnp.einsum("oabcr,pqusr->oapbqcus", shaped, octant_grid)
    return children.reshape(orbits, -1, rank_width)


def couple_lists(moments, sources, coupling, scale):
    orbits, node_count, rank_width = moments.shape

    def one_slot(running, inputs):
        column, matrix = inputs
        picked = jnp.take(moments, column, axis=1).astype(jnp.float32)
        return running + jnp.einsum("ons,rs->onr", picked, matrix.astype(jnp.float32)), None

    start = jnp.zeros((orbits, sources.shape[0], rank_width), jnp.float32)
    running, _ = lax.scan(one_slot, start, (sources.T, coupling))
    return scale * running


def near_sum(density, sources, near_table):
    orbits, node_count, points = density.shape

    def one_slot(running, inputs):
        column, matrix = inputs
        picked = jnp.take(density, column, axis=1).reshape(orbits * node_count, points)
        return running + jnp.dot(picked, matrix.T, preferred_element_type=jnp.float32), None

    start = jnp.zeros((orbits * node_count, points), jnp.float32)
    running, _ = lax.scan(one_slot, start, (sources.T, near_table))
    return running.reshape(orbits, node_count, points)


def shifted(values, offset):
    node_count = values.shape[1]
    if abs(offset) >= node_count:
        return jnp.zeros_like(values)
    empty = jnp.zeros((values.shape[0], abs(offset), values.shape[2]), values.dtype)
    if offset > 0:
        return jnp.concatenate([values[:, offset:], empty], axis=1)
    return jnp.concatenate([empty, values[:, :offset]], axis=1)


def coarse_couple(moments, coarse_coupling, scale):
    values = moments.astype(jnp.float32)
    node_count = values.shape[1]
    odd_rows = (jnp.arange(node_count) % 2).astype(jnp.float32)[None, :, None]
    even_rows = 1.0 - odd_rows

    def apply_matrix(which, offset):
        return jnp.einsum("ons,rs->onr", shifted(values, offset), coarse_coupling[which].astype(jnp.float32))

    running = apply_matrix(1, -2) + apply_matrix(2, 2) + even_rows * apply_matrix(3, 3) + odd_rows * apply_matrix(0, -3)
    return scale * running


def coarse_up(moments, pair_transfer):
    orbits, node_count, rank_width = moments.shape
    if node_count % 2 == 1:
        moments = jnp.concatenate([moments, jnp.zeros((orbits, 1, rank_width), moments.dtype)], axis=1)
    shaped = moments.reshape(orbits, -1, 2, rank_width).astype(jnp.float32)
    return jnp.einsum("oaps,psr->oar", shaped, pair_transfer.astype(jnp.float32)).astype(jnp.bfloat16)


def coarse_down(coeffs, pair_transfer, node_count):
    children = jnp.einsum("oar,psr->oaps", coeffs.astype(jnp.float32), pair_transfer.astype(jnp.float32))
    return children.reshape(coeffs.shape[0], -1, coeffs.shape[2])[:, :node_count]


def coarse_tree(cube_moments, coarse_coupling, pair_transfer):
    levels = [cube_moments]
    while levels[-1].shape[1] > 1:
        levels.append(coarse_up(levels[-1], pair_transfer))
    top_level = len(levels) - 1
    coeffs = coarse_couple(levels[top_level], coarse_coupling, 0.5 ** (3 + top_level)).astype(jnp.bfloat16)
    for depth_level in range(top_level - 1, -1, -1):
        pushed = coarse_down(coeffs, pair_transfer, levels[depth_level].shape[1])
        coupled = coarse_couple(levels[depth_level], coarse_coupling, 0.5 ** (3 + depth_level))
        coeffs = (coupled + pushed).astype(jnp.bfloat16)
    return coeffs


def reference(orbitals, near_source, far_leaf, far_mid, far_top, leaf_basis, near_table, transfer, coupling, pair_transfer, coarse_coupling):
    density = (orbitals * orbitals).astype(jnp.bfloat16)
    leaf_moments = jnp.einsum("olp,rp->olr", density.astype(jnp.float32), leaf_basis.astype(jnp.float32)).astype(jnp.bfloat16)
    mid_moments = octant_up(leaf_moments, SIDE, transfer)
    top_moments = octant_up(mid_moments, SIDE // 2, transfer)
    cube_moments = octant_up(top_moments, SIDE // 4, transfer)
    cube_coeffs = coarse_tree(cube_moments, coarse_coupling, pair_transfer)
    top_coeffs = (couple_lists(top_moments, far_top, coupling, 0.25) + octant_down(cube_coeffs, SIDE // 8, transfer)).astype(jnp.bfloat16)
    mid_coeffs = (couple_lists(mid_moments, far_mid, coupling, 0.5) + octant_down(top_coeffs, SIDE // 4, transfer)).astype(jnp.bfloat16)
    leaf_coeffs = (couple_lists(leaf_moments, far_leaf, coupling, 1.0) + octant_down(mid_coeffs, SIDE // 2, transfer)).astype(jnp.bfloat16)
    near_field = near_sum(density, near_source, near_table)
    far_field = jnp.einsum("olr,rp->olp", leaf_coeffs.astype(jnp.float32), leaf_basis.astype(jnp.float32))
    potential = near_field + far_field
    hartree = jnp.sum(potential, axis=0)
    return orbitals - relax_step * (hartree[None] - potential) * orbitals
```

```python
import jax
import jax.numpy as jnp
from jax import lax
from jax.experimental import pallas as pl
from jax.experimental.pallas import tpu as pltpu
from jax.sharding import PartitionSpec as P

BF = jnp.bfloat16
F32 = jnp.float32
NN = (((1,), (0,)), ((), ()))
NT = (((1,), (1,)), ((), ()))
RELAX_STEP = 0.1
PARAMS = pltpu.CompilerParams(vmem_limit_bytes=56 << 20)


def dot(a, b, dims=NN):
    return lax.dot_general(a, b, dims, preferred_element_type=F32)


def iota(shape, dim):
    return lax.broadcasted_iota(jnp.int32, shape, dim)


def ones_where(mask):
    return jnp.where(mask, 1.0, 0.0).astype(BF)


def one_hot(column, rows, width):
    return ones_where(iota((rows, width), 1) == column)


def twice(matrices):
    zero = jnp.zeros_like(matrices)
    top = jnp.concatenate([matrices, zero], axis=-1)
    low = jnp.concatenate([zero, matrices], axis=-1)
    return jnp.concatenate([top, low], axis=-2)


def octant_picker(parents, half, width):
    row, col = iota((8 * parents, width), 0), iota((8 * parents, width), 1)
    octant, b = row // parents, row % parents
    z, y, x = b // (half * half), (b // half) % half, b % half
    dz, dy, dx = octant // 4, (octant // 2) % 2, octant % 2
    side = 2 * half
    child = ((2 * z + dz) * side + 2 * y + dy) * side + 2 * x + dx
    return ones_where(child == col)


def merge_up(picked, parents, transfer_ref):
    total = None
    for octant in range(8):
        part = dot(picked[octant * parents : (octant + 1) * parents], transfer_ref[octant])
        total = part if total is None else total + part
    return total.astype(BF)


def moments_kernel(
    orb_ref, basis_ref, transfer_ref, dens_ref, leaf_ref, mid_ref, top_ref, cube_ref, head_ref, tail_ref
):
    step = pl.program_id(0)
    for o in range(2):
        values = orb_ref[o]
        dens_ref[:, o * 256 : (o + 1) * 256] = (values * values).astype(BF)
    leaf = dot(dens_ref[...], basis_ref[...], NT).astype(BF)
    leaf_ref[...] = leaf
    picked = dot(octant_picker(32, 4, 256), leaf).astype(BF)
    mid = merge_up(picked, 32, transfer_ref)
    mid_ref[pl.ds(pl.multiple_of(step * 32, 32), 32), :] = mid

    @pl.when(step == 0)
    def _():
        head_ref[0:192, :] = leaf[0:192]

    @pl.when(step == 3)
    def _():
        tail_ref[0:192, :] = leaf[64:256]
        mids = mid_ref[...]
        top = merge_up(dot(octant_picker(16, 2, 128), mids).astype(BF), 16, transfer_ref)
        top_ref[...] = top
        cube_ref[...] = merge_up(dot(octant_picker(16, 1, 16), top).astype(BF), 16, transfer_ref)
        head_ref[192:240, :] = mids[0:48]
        tail_ref[192:240, :] = mids[80:128]
        head_ref[240:256, :] = top
        tail_ref[240:256, :] = top


def moments(orbitals, basis2, transfer2):
    whole = lambda *shape: pl.BlockSpec(shape, lambda c: (0,) * len(shape))
    shape = lambda *s: jax.ShapeDtypeStruct(s, BF)
    return pl.pallas_call(
        moments_kernel,
        grid=(4,),
        in_specs=[pl.BlockSpec((2, 256, 256), lambda c: (0, c, 0)), whole(128, 512), whole(8, 128, 128)],
        out_specs=[
            pl.BlockSpec((256, 512), lambda c: (c, 0)),
            pl.BlockSpec((256, 128), lambda c: (c, 0)),
            whole(128, 128),
            whole(16, 128),
            whole(16, 128),
            whole(256, 128),
            whole(256, 128),
        ],
        out_shape=[
            shape(1024, 512),
            shape(1024, 128),
            shape(128, 128),
            shape(16, 128),
            shape(16, 128),
            shape(256, 128),
            shape(256, 128),
        ],
        compiler_params=PARAMS,
        cost_estimate=pl.CostEstimate(flops=400_000_000, bytes_accessed=4 << 20, transcendentals=0),
        name="moments",
    )(orbitals, basis2, transfer2)


def near_kernel(
    source_ref, prev_ref, dens_ref, next_ref, table_ref, near_ref, sum_ref, ext_ref, hot_ref, pick_ref
):
    step = pl.program_id(0)

    @pl.when(step == 0)
    def _():
        ext_ref[0:64, :] = prev_ref[...]
        ext_ref[64:1088, :] = dens_ref[...]
        ext_ref[1088:1152, :] = next_ref[...]

    for part in range(2):
        place = (source_ref[part * 128 : (part + 1) * 128, :] + (64 + 128 * part)) & 255
        for k in range(27):
            hot_ref[k * 128 : (k + 1) * 128, :] = one_hot(place[:, k : k + 1], 128, 256)
        base = pl.multiple_of(step * 256 + part * 128, 128)
        for o in range(2):
            rows = ext_ref[pl.ds(base, 256), o * 256 : (o + 1) * 256]
            at = o * 256 + part * 128
            for first in range(0, 27, 9):
                picked = dot(hot_ref[first * 128 : (first + 9) * 128, :], rows).astype(BF)
                for k in range(9):
                    pick_ref[at : at + 128, (first + k) * 256 : (first + k + 1) * 256] = picked[
                        k * 128 : (k + 1) * 128
                    ]
    total = None
    for k in range(27):
        part = dot(pick_ref[:, k * 256 : (k + 1) * 256], table_ref[k], NT)
        total = part if total is None else total + part
    near_ref[:, :256] = total[:256]
    near_ref[:, 256:] = total[256:]
    sum_ref[...] = (total[:256] + total[256:]).astype(BF)


def near_field(sources, prev, density, after, table):
    whole = lambda *shape: pl.BlockSpec(shape, lambda c: (0,) * len(shape))
    rows = lambda *shape: pl.BlockSpec(shape, lambda c: (c, 0))
    return pl.pallas_call(
        near_kernel,
        grid=(4,),
        in_specs=[rows(256, 27), whole(64, 512), whole(1024, 512), whole(64, 512), whole(27, 256, 256)],
        out_specs=[rows(256, 512), rows(256, 256)],
        out_shape=[jax.ShapeDtypeStruct((1024, 512), F32), jax.ShapeDtypeStruct((1024, 256), BF)],
        scratch_shapes=[
            pltpu.VMEM((1152, 512), BF),
            pltpu.VMEM((27 * 128, 256), BF),
            pltpu.VMEM((512, 27 * 256), BF),
        ],
        compiler_params=PARAMS,
        cost_estimate=pl.CostEstimate(flops=15_000_000_000, bytes_accessed=8 << 20, transcendentals=0),
        name="near",
    )(sources, prev, density, after, table)


def far_kernel(
    leaf_list, mid_list, top_list, prev_ref, leaf_ref, mid_ref, top_ref, next_ref, coupling_ref,
    out_ref, ext_ref, midx_ref, topx_ref, weight_ref, hot_ref, pick_ref,
):
    step = pl.program_id(0)
    device = lax.axis_index("space")

    @pl.when(step == 0)
    def _():
        ext_ref[0:192, :] = prev_ref[0:192]
        ext_ref[192:1216, :] = leaf_ref[...]
        ext_ref[1216:1408, :] = next_ref[0:192]
        midx_ref[0:48, :] = prev_ref[192:240]
        midx_ref[48:176, :] = mid_ref[...]
        midx_ref[176:224, :] = next_ref[192:240]
        midx_ref[224:256, :] = jnp.zeros((32, 128), BF)
        topx_ref[0:16, :] = prev_ref[240:256]
        topx_ref[16:32, :] = top_ref[...]
        topx_ref[32:48, :] = next_ref[240:256]
        topx_ref[48:128, :] = jnp.zeros((80, 128), BF)
        zero = jnp.zeros((64, 64), BF)
        for k in range(108):
            matrix = coupling_ref[k]
            weight_ref[0:64, k * 128 : (k + 1) * 128] = jnp.concatenate([matrix, zero], axis=1)
            weight_ref[64:128, k * 128 : (k + 1) * 128] = jnp.concatenate([zero, matrix], axis=1)

    def pick(place, rows, at, table):
        width = table.shape[0]
        for k in range(108):
            hot_ref[k * rows : (k + 1) * rows, :width] = one_hot(place[:, k : k + 1], rows, width)
        for first in range(0, 108, 12):
            picked = dot(hot_ref[first * rows : (first + 12) * rows, :width], table).astype(BF)
            for k in range(12):
                pick_ref[at : at + rows, (first + k) * 128 : (first + k + 1) * 128] = picked[
                    k * rows : (k + 1) * rows
                ]

    @pl.when(step < 4)
    def _():
        for part in range(4):
            base = pl.multiple_of(step * 256 + part * 64, 64)
            offset = (leaf_list[part * 64 : (part + 1) * 64, :] - base + 192) & 1023
            place = jnp.where(offset < 128, offset, offset - 192)
            table = jnp.concatenate([ext_ref[pl.ds(base, 128), :], ext_ref[pl.ds(base + 320, 128), :]], axis=0)
            pick(place, 64, part * 64, table)

    @pl.when(step == 4)
    def _():
        for part in range(2):
            place = mid_list[part * 64 : (part + 1) * 64, :] - (device * 128 - 48)
            pick(place, 64, part * 64, midx_ref[...])
        pick(top_list[...] - (device * 16 - 16), 16, 128, topx_ref[...])

    out_ref[...] = dot(pick_ref[...], weight_ref[...], NT)


def far_sums(far_leaf, far_mid, far_top, prev, leaf, mid, top, after, coupling):
    whole = lambda *shape: pl.BlockSpec(shape, lambda c: (0,) * len(shape))
    return pl.pallas_call(
        far_kernel,
        grid=(5,),
        in_specs=[
            pl.BlockSpec((256, 108), lambda c: (jnp.minimum(c, 3), 0)),
            whole(128, 108),
            whole(16, 108),
            whole(256, 128),
            whole(1024, 128),
            whole(128, 128),
            whole(16, 128),
            whole(256, 128),
            whole(108, 64, 64),
        ],
        out_specs=pl.BlockSpec((256, 128), lambda c: (c, 0)),
        out_shape=jax.ShapeDtypeStruct((1280, 128), F32),
        scratch_shapes=[
            pltpu.VMEM((1408, 128), BF),
            pltpu.VMEM((256, 128), BF),
            pltpu.VMEM((128, 128), BF),
            pltpu.VMEM((128, 108 * 128), BF),
            pltpu.VMEM((108 * 64, 256), BF),
            pltpu.VMEM((256, 108 * 128), BF),
        ],
        compiler_params=PARAMS,
        cost_estimate=pl.CostEstimate(flops=20_000_000_000, bytes_accessed=4 << 20, transcendentals=0),
        name="far",
    )(far_leaf, far_mid, far_top, prev, leaf, mid, top, after, coupling)


def tree_kernel(cube_ref, pair_ref, coarse_ref, transfer_ref, far_ref, coeff_ref, sum_ref):
    device = lax.axis_index("space")
    row, col = iota((64, 64), 0), iota((64, 64), 1)
    child = [ones_where(col == 2 * row + p) for p in range(2)]
    mother = [ones_where((col == row // 2) & (row % 2 == p)) for p in range(2)]
    shift = [
        ones_where((col == row - 3) & (row % 2 == 1)),
        ones_where(col == row - 2),
        ones_where(col == row + 2),
        ones_where((col == row + 3) & (row % 2 == 0)),
    ]
    levels = [cube_ref[...]]
    for _ in range(6):
        total = None
        for p in range(2):
            part = dot(dot(child[p], levels[-1]).astype(BF), pair_ref[p])
            total = part if total is None else total + part
        levels.append(total.astype(BF))
    coeffs = None
    for depth in range(6, -1, -1):
        total = None
        for w in range(4):
            part = dot(dot(shift[w], levels[depth]).astype(BF), coarse_ref[w], NT)
            total = part if total is None else total + part
        total = total * (0.5 ** (3 + depth))
        if coeffs is not None:
            for p in range(2):
                total = total + dot(dot(mother[p], coeffs).astype(BF), pair_ref[p], NT)
        coeffs = total.astype(BF)

    def split_down(coeffs, parents, children, half, first):
        row, col = iota((children, parents), 0), iota((children, parents), 1)
        side = 2 * half
        z, y, x = row // (side * side), (row // side) % side, row % side
        parent = ((z // 2) * half + y // 2) * half + x // 2 + first
        pulled = dot(ones_where(col == parent), coeffs).astype(BF)
        r = iota((children, 128), 0)
        octant = 4 * ((r // (side * side)) % 2) + 2 * ((r // side) % 2) + r % 2
        total = None
        for o in range(8):
            part = dot(jnp.where(octant == o, pulled, jnp.zeros_like(pulled)), transfer_ref[o], NT)
            total = part if total is None else total + part
        return total

    top = 0.25 * far_ref[1152:1168] + split_down(coeffs, 64, 16, 1, 2 * device)
    mid = 0.5 * far_ref[1024:1152] + split_down(top.astype(BF), 16, 128, 2, 0)
    leaf = far_ref[0:1024] + split_down(mid.astype(BF), 128, 1024, 4, 0)
    leaf = leaf.astype(BF)
    coeff_ref[...] = leaf
    wide = leaf.astype(F32)
    sum_ref[...] = (wide[:, :64] + wide[:, 64:]).astype(BF)


def tree_down(cubes, pair2, coarse2, transfer2, far):
    return pl.pallas_call(
        tree_kernel,
        out_shape=[jax.ShapeDtypeStruct((1024, 128), BF), jax.ShapeDtypeStruct((1024, 64), BF)],
        compiler_params=PARAMS,
        cost_estimate=pl.CostEstimate(flops=600_000_000, bytes_accessed=2 << 20, transcendentals=0),
        name="tree",
    )(cubes, pair2, coarse2, transfer2, far)


def relax_kernel(orb_ref, near_ref, coeff_ref, near_sum_ref, coeff_sum_ref, basis2_ref, basis_ref, out_ref):
    potential = near_ref[...] + dot(coeff_ref[...], basis2_ref[...])
    hartree = near_sum_ref[...].astype(F32) + dot(coeff_sum_ref[...], basis_ref[...])
    for o in range(2):
        values = orb_ref[o]
        out_ref[o] = values - RELAX_STEP * (hartree - potential[:, o * 256 : (o + 1) * 256]) * values


def relax(orbitals, near, coeffs, near_sum, coeff_sum, basis2, basis):
    whole = lambda *shape: pl.BlockSpec(shape, lambda c: (0,) * len(shape))
    rows = lambda *shape: pl.BlockSpec(shape, lambda c: (c, 0))
    block = pl.BlockSpec((2, 256, 256), lambda c: (0, c, 0))
    return pl.pallas_call(
        relax_kernel,
        grid=(4,),
        in_specs=[block, rows(256, 512), rows(256, 128), rows(256, 256), rows(256, 64), whole(128, 512), whole(64, 256)],
        out_specs=block,
        out_shape=jax.ShapeDtypeStruct((2, 1024, 256), F32),
        compiler_params=PARAMS,
        cost_estimate=pl.CostEstimate(flops=300_000_000, bytes_accessed=8 << 20, transcendentals=0),
        name="relax",
    )(orbitals, near, coeffs, near_sum, coeff_sum, basis2, basis)


def shards(
    orbitals, near_source, far_leaf, far_mid, far_top, leaf_basis, near_table, transfer, coupling, pair_transfer,
    coarse_coupling,
):
    count = lax.axis_size("space")
    to_next = [(i, i + 1) for i in range(count - 1)]
    to_prev = [(i + 1, i) for i in range(count - 1)]
    basis2 = twice(leaf_basis)
    small = twice(jnp.concatenate([transfer, pair_transfer, coarse_coupling], axis=0))
    transfer2, pair2, coarse2 = small[0:8], small[8:10], small[10:14]
    density, leaf, mid, top, cube, head, tail = moments(orbitals, basis2, transfer2)
    dens_prev = lax.ppermute(density[960:1024], "space", to_next)
    dens_next = lax.ppermute(density[0:64], "space", to_prev)
    far_prev = lax.ppermute(tail, "space", to_next)
    far_next = lax.ppermute(head, "space", to_prev)
    cubes = lax.all_gather(cube[0:2], "space", axis=0, tiled=True)
    near, near_part = near_field(near_source, dens_prev, density, dens_next, near_table)
    near_sum = lax.psum(near_part, "orb")
    far = far_sums(far_leaf, far_mid, far_top, far_prev, leaf, mid, top, far_next, coupling)
    coeffs, coeff_part = tree_down(cubes, pair2, coarse2, transfer2, far)
    near_sum, coeff_part = lax.optimization_barrier((near_sum, coeff_part))
    coeff_sum = lax.psum(coeff_part, "orb")
    return relax(orbitals, near, coeffs, near_sum, coeff_sum, basis2, leaf_basis)


def solution(mesh):
    placed = (P("orb", "space", None),) + (P("space", None),) * 4 + (P(),) * 6
    return jax.shard_map(
        shards, mesh=mesh, in_specs=placed, out_specs=P("orb", "space", None), check_vma=False
    )
```

```python
import jax
import jax.numpy as jnp
from jax import lax
from jax.experimental import pallas as pl
from jax.experimental.pallas import tpu as pltpu
from jax.sharding import PartitionSpec as P

BF = jnp.bfloat16
F32 = jnp.float32
NN = (((1,), (0,)), ((), ()))
NT = (((1,), (1,)), ((), ()))
RELAX_STEP = 0.1
MESH = pl.DeviceIdType.MESH
PARAMS = pltpu.CompilerParams(vmem_limit_bytes=56 << 20)


def dot(a, b, dims=NN):
    return lax.dot_general(a, b, dims, preferred_element_type=F32)


def iota(shape, dim):
    return lax.broadcasted_iota(jnp.int32, shape, dim)


def ones_where(mask):
    return jnp.where(mask, 1.0, 0.0).astype(BF)


def one_hot(column, rows, width):
    return ones_where(iota((rows, width), 1) == column)


def octant_picker(parents, half, width):
    row, col = iota((8 * parents, width), 0), iota((8 * parents, width), 1)
    octant, b = row // parents, row % parents
    z, y, x = b // (half * half), (b // half) % half, b % half
    dz, dy, dx = octant // 4, (octant // 2) % 2, octant % 2
    side = 2 * half
    child = ((2 * z + dz) * side + 2 * y + dy) * side + 2 * x + dx
    return ones_where(child == col)


def merge_up(picked, parents, transfer_ref):
    total = None
    for octant in range(8):
        part = dot(picked[octant * parents : (octant + 1) * parents], transfer_ref[octant])
        total = part if total is None else total + part
    return total.astype(BF)


def spread(matrix):
    zero = jnp.zeros_like(matrix)
    top = jnp.concatenate([matrix, zero], axis=1)
    return jnp.concatenate([top, jnp.concatenate([zero, matrix], axis=1)], axis=0)


def spread_basis(basis_ref, basis2_ref):
    basis2_ref[...] = jnp.zeros((128, 512), BF)
    basis2_ref[0:64, 0:256] = basis_ref[...]
    basis2_ref[64:128, 256:512] = basis_ref[...]


def moments_kernel(
    orb_ref, basis_ref, matrix_ref,
    dens_ref, leaf_ref, mid_ref, top_ref, dens_prev, dens_next, far_prev, far_next, cubes_ref,
    basis2_ref, transfer_ref, edge_ref, rim_ref, cube_ref, send, recv, cube_send, cube_recv, own_sem,
):
    step = pl.program_id(0)
    me, orb = lax.axis_index("space"), lax.axis_index("orb")
    count = lax.axis_size("space")
    after, before = lax.rem(me + 1, count), lax.rem(me + count - 1, count)

    def halo(number, source, target, device):
        return pltpu.make_async_remote_copy(
            src_ref=source,
            dst_ref=target,
            send_sem=send.at[number],
            recv_sem=recv.at[number],
            device_id=(device, orb),
            device_id_type=MESH,
        )

    halos = [
        halo(0, edge_ref.at[0], dens_next, before),
        halo(1, edge_ref.at[1], dens_prev, after),
        halo(2, rim_ref.at[0], far_next, before),
        halo(3, rim_ref.at[1], far_prev, after),
    ]

    def cube_copy(other, owner):
        return pltpu.make_async_remote_copy(
            src_ref=cube_ref,
            dst_ref=cubes_ref.at[pl.ds(pl.multiple_of(owner * 16, 16), 16)],
            send_sem=cube_send.at[other],
            recv_sem=cube_recv.at[owner],
            device_id=(other, orb),
            device_id_type=MESH,
        )

    @pl.when(step == 0)
    def _():
        barrier = pltpu.get_barrier_semaphore()

        def greet(i, _):
            other = lax.rem(me + i, count)
            pl.semaphore_signal(barrier, inc=1, device_id=(other, orb), device_id_type=MESH)
            return 0

        lax.fori_loop(1, count, greet, 0)
        spread_basis(basis_ref, basis2_ref)
        for octant in range(8):
            transfer_ref[octant] = spread(matrix_ref[octant])

    for o in range(2):
        values = orb_ref[o]
        dens_ref[:, o * 256 : (o + 1) * 256] = (values * values).astype(BF)
    leaf = dot(dens_ref[...], basis2_ref[...], NT).astype(BF)
    leaf_ref[...] = leaf
    picked = dot(octant_picker(32, 4, 256), leaf).astype(BF)
    mid = merge_up(picked, 32, transfer_ref)
    mid_ref[pl.ds(pl.multiple_of(step * 32, 32), 32), :] = mid

    @pl.when(step == 0)
    def _():
        rim_ref[0, 0:192, :] = leaf[0:192]
        edge_ref[0] = dens_ref[0:64, :]
        pl.semaphore_wait(pltpu.get_barrier_semaphore(), count - 1)
        halos[0].start()

    @pl.when(step == 3)
    def _():
        edge_ref[1] = dens_ref[192:256, :]
        halos[1].start()
        rim_ref[1, 0:192, :] = leaf[64:256]
        mids = mid_ref[...]
        top = merge_up(dot(octant_picker(16, 2, 128), mids).astype(BF), 16, transfer_ref)
        top_ref[...] = top
        rim_ref[0, 192:240, :] = mids[0:48]
        rim_ref[1, 192:240, :] = mids[80:128]
        rim_ref[0, 240:256, :] = top
        rim_ref[1, 240:256, :] = top
        halos[2].start()
        halos[3].start()
        cube_ref[...] = merge_up(dot(octant_picker(16, 1, 16), top).astype(BF), 16, transfer_ref)

        def send_cube(i, _):
            cube_copy(lax.rem(me + i, count), me).start()
            return 0

        lax.fori_loop(1, count, send_cube, 0)
        own = pltpu.make_async_copy(
            cube_ref, cubes_ref.at[pl.ds(pl.multiple_of(me * 16, 16), 16)], own_sem
        )
        own.start()
        own.wait()
        for copy in halos:
            copy.wait()

        def wait_cube(i, _):
            other = lax.rem(me + i, count)
            cube_copy(other, me).wait_send()
            cube_copy(other, other).wait_recv()
            return 0

        lax.fori_loop(1, count, wait_cube, 0)


def moments(orbitals, basis, transfer):
    whole = lambda *shape: pl.BlockSpec(shape, lambda c: (0,) * len(shape))
    shape = lambda *s: jax.ShapeDtypeStruct(s, BF)
    landing = pl.BlockSpec(memory_space=pl.ANY)
    count = lax.axis_size("space")
    return pl.pallas_call(
        moments_kernel,
        grid=(4,),
        in_specs=[pl.BlockSpec((2, 256, 256), lambda c: (0, c, 0)), whole(64, 256), whole(8, 64, 64)],
        out_specs=[
            pl.BlockSpec((256, 512), lambda c: (c, 0)),
            pl.BlockSpec((256, 128), lambda c: (c, 0)),
            whole(128, 128),
            whole(16, 128),
            landing,
            landing,
            landing,
            landing,
            landing,
        ],
        out_shape=[
            shape(1024, 512),
            shape(1024, 128),
            shape(128, 128),
            shape(16, 128),
            shape(64, 512),
            shape(64, 512),
            shape(256, 128),
            shape(256, 128),
            shape(count * 16, 128),
        ],
        scratch_shapes=[
            pltpu.VMEM((128, 512), BF),
            pltpu.VMEM((8, 128, 128), BF),
            pltpu.VMEM((2, 64, 512), BF),
            pltpu.VMEM((2, 256, 128), BF),
            pltpu.VMEM((16, 128), BF),
            pltpu.SemaphoreType.DMA((4,)),
            pltpu.SemaphoreType.DMA((4,)),
            pltpu.SemaphoreType.DMA((count,)),
            pltpu.SemaphoreType.DMA((count,)),
            pltpu.SemaphoreType.DMA,
        ],
        compiler_params=pltpu.CompilerParams(
            vmem_limit_bytes=40 << 20, collective_id=0, has_side_effects=True
        ),
        cost_estimate=pl.CostEstimate(flops=400_000_000, bytes_accessed=4 << 20, transcendentals=0),
        name="moments",
    )(orbitals, basis, transfer)


def near_kernel(
    source_ref, prev_ref, dens_ref, next_ref, table_ref, near_ref, sum_ref, ext_ref, hot_ref, pick_ref
):
    step = pl.program_id(0)

    @pl.when(step == 0)
    def _():
        ext_ref[0:64, :] = prev_ref[...]
        ext_ref[64:1088, :] = dens_ref[...]
        ext_ref[1088:1152, :] = next_ref[...]

    for part in range(2):
        place = (source_ref[part * 128 : (part + 1) * 128, :] + (64 + 128 * part)) & 255
        for k in range(27):
            hot_ref[k * 128 : (k + 1) * 128, :] = one_hot(place[:, k : k + 1], 128, 256)
        base = pl.multiple_of(step * 256 + part * 128, 128)
        for o in range(2):
            rows = ext_ref[pl.ds(base, 256), o * 256 : (o + 1) * 256]
            at = o * 256 + part * 128
            for first in range(0, 27, 9):
                picked = dot(hot_ref[first * 128 : (first + 9) * 128, :], rows).astype(BF)
                for k in range(9):
                    pick_ref[at : at + 128, (first + k) * 256 : (first + k + 1) * 256] = picked[
                        k * 128 : (k + 1) * 128
                    ]
    total = None
    for k in range(27):
        part = dot(pick_ref[:, k * 256 : (k + 1) * 256], table_ref[k], NT)
        total = part if total is None else total + part
    near_ref[:, :256] = total[:256]
    near_ref[:, 256:] = total[256:]
    sum_ref[...] = (total[:256] + total[256:]).astype(BF)


def near_field(sources, prev, density, after, table):
    whole = lambda *shape: pl.BlockSpec(shape, lambda c: (0,) * len(shape))
    rows = lambda *shape: pl.BlockSpec(shape, lambda c: (c, 0))
    return pl.pallas_call(
        near_kernel,
        grid=(4,),
        in_specs=[rows(256, 27), whole(64, 512), whole(1024, 512), whole(64, 512), whole(27, 256, 256)],
        out_specs=[rows(256, 512), rows(256, 256)],
        out_shape=[jax.ShapeDtypeStruct((1024, 512), F32), jax.ShapeDtypeStruct((1024, 256), BF)],
        scratch_shapes=[
            pltpu.VMEM((1152, 512), BF),
            pltpu.VMEM((27 * 128, 256), BF),
            pltpu.VMEM((512, 27 * 256), BF),
        ],
        compiler_params=PARAMS,
        cost_estimate=pl.CostEstimate(flops=15_000_000_000, bytes_accessed=8 << 20, transcendentals=0),
        name="near",
    )(sources, prev, density, after, table)


def far_kernel(
    leaf_list, mid_list, top_list, prev_ref, leaf_ref, mid_ref, top_ref, next_ref, coupling_ref,
    out_ref, ext_ref, midx_ref, topx_ref, weight_ref, hot_ref, pick_ref,
):
    step = pl.program_id(0)
    device = lax.axis_index("space")

    @pl.when(step == 0)
    def _():
        ext_ref[0:192, :] = prev_ref[0:192]
        ext_ref[192:1216, :] = leaf_ref[...]
        ext_ref[1216:1408, :] = next_ref[0:192]
        midx_ref[0:48, :] = prev_ref[192:240]
        midx_ref[48:176, :] = mid_ref[...]
        midx_ref[176:224, :] = next_ref[192:240]
        midx_ref[224:256, :] = jnp.zeros((32, 128), BF)
        topx_ref[0:16, :] = prev_ref[240:256]
        topx_ref[16:32, :] = top_ref[...]
        topx_ref[32:48, :] = next_ref[240:256]
        topx_ref[48:128, :] = jnp.zeros((80, 128), BF)
        zero = jnp.zeros((64, 64), BF)
        for k in range(108):
            matrix = coupling_ref[k]
            weight_ref[0:64, k * 128 : (k + 1) * 128] = jnp.concatenate([matrix, zero], axis=1)
            weight_ref[64:128, k * 128 : (k + 1) * 128] = jnp.concatenate([zero, matrix], axis=1)

    def pick(place, rows, at, table):
        width = table.shape[0]
        for k in range(108):
            hot_ref[k * rows : (k + 1) * rows, :width] = one_hot(place[:, k : k + 1], rows, width)
        for first in range(0, 108, 12):
            picked = dot(hot_ref[first * rows : (first + 12) * rows, :width], table).astype(BF)
            for k in range(12):
                pick_ref[at : at + rows, (first + k) * 128 : (first + k + 1) * 128] = picked[
                    k * rows : (k + 1) * rows
                ]

    @pl.when(step < 4)
    def _():
        for part in range(4):
            base = pl.multiple_of(step * 256 + part * 64, 64)
            offset = (leaf_list[part * 64 : (part + 1) * 64, :] - base + 192) & 1023
            place = jnp.where(offset < 128, offset, offset - 192)
            table = jnp.concatenate([ext_ref[pl.ds(base, 128), :], ext_ref[pl.ds(base + 320, 128), :]], axis=0)
            pick(place, 64, part * 64, table)

    @pl.when(step == 4)
    def _():
        for part in range(2):
            place = mid_list[part * 64 : (part + 1) * 64, :] - (device * 128 - 48)
            pick(place, 64, part * 64, midx_ref[...])
        pick(top_list[...] - (device * 16 - 16), 16, 128, topx_ref[...])

    out_ref[...] = dot(pick_ref[...], weight_ref[...], NT)


def far_sums(far_leaf, far_mid, far_top, prev, leaf, mid, top, after, coupling):
    whole = lambda *shape: pl.BlockSpec(shape, lambda c: (0,) * len(shape))
    return pl.pallas_call(
        far_kernel,
        grid=(5,),
        in_specs=[
            pl.BlockSpec((256, 108), lambda c: (jnp.minimum(c, 3), 0)),
            whole(128, 108),
            whole(16, 108),
            whole(256, 128),
            whole(1024, 128),
            whole(128, 128),
            whole(16, 128),
            whole(256, 128),
            whole(108, 64, 64),
        ],
        out_specs=pl.BlockSpec((256, 128), lambda c: (c, 0)),
        out_shape=jax.ShapeDtypeStruct((1280, 128), F32),
        scratch_shapes=[
            pltpu.VMEM((1408, 128), BF),
            pltpu.VMEM((256, 128), BF),
            pltpu.VMEM((128, 128), BF),
            pltpu.VMEM((128, 108 * 128), BF),
            pltpu.VMEM((108 * 64, 256), BF),
            pltpu.VMEM((256, 108 * 128), BF),
        ],
        compiler_params=PARAMS,
        cost_estimate=pl.CostEstimate(flops=20_000_000_000, bytes_accessed=4 << 20, transcendentals=0),
        name="far",
    )(far_leaf, far_mid, far_top, prev, leaf, mid, top, after, coupling)


def tree_kernel(
    cube_ref, pair_in, coarse_in, transfer_in, far_ref,
    coeff_ref, sum_ref,
    pair_ref, coarse_ref, transfer_ref, part_ref, other_ref, send, recv,
):
    device, orb = lax.axis_index("space"), lax.axis_index("orb")
    orbs = lax.axis_size("orb")
    barrier = pltpu.get_barrier_semaphore()
    for away in range(1, orbs):
        other = lax.rem(orb + away, orbs)
        pl.semaphore_signal(barrier, inc=1, device_id=(device, other), device_id_type=MESH)
    for given, kept in ((pair_in, pair_ref), (coarse_in, coarse_ref), (transfer_in, transfer_ref)):
        for i in range(given.shape[0]):
            kept[i] = spread(given[i])
    row, col = iota((64, cube_ref.shape[0]), 0), iota((64, cube_ref.shape[0]), 1)
    cubes = dot(ones_where(col == 16 * (row // 2) + row % 2), cube_ref[...]).astype(BF)
    row, col = iota((64, 64), 0), iota((64, 64), 1)
    child = [ones_where(col == 2 * row + p) for p in range(2)]
    mother = [ones_where((col == row // 2) & (row % 2 == p)) for p in range(2)]
    shift = [
        ones_where((col == row - 3) & (row % 2 == 1)),
        ones_where(col == row - 2),
        ones_where(col == row + 2),
        ones_where((col == row + 3) & (row % 2 == 0)),
    ]
    levels = [cubes]
    for _ in range(6):
        total = None
        for p in range(2):
            part = dot(dot(child[p], levels[-1]).astype(BF), pair_ref[p])
            total = part if total is None else total + part
        levels.append(total.astype(BF))
    coeffs = None
    for depth in range(6, -1, -1):
        total = None
        for w in range(4):
            part = dot(dot(shift[w], levels[depth]).astype(BF), coarse_ref[w], NT)
            total = part if total is None else total + part
        total = total * (0.5 ** (3 + depth))
        if coeffs is not None:
            for p in range(2):
                total = total + dot(dot(mother[p], coeffs).astype(BF), pair_ref[p], NT)
        coeffs = total.astype(BF)

    def split_down(coeffs, children, half, first, start, rows):
        parents = coeffs.shape[0]
        side = 2 * half
        row, col = iota((rows, parents), 0) + start, iota((rows, parents), 1)
        z, y, x = row // (side * side), (row // side) % side, row % side
        parent = ((z // 2) * half + y // 2) * half + x // 2 + first
        pulled = dot(ones_where(col == parent), coeffs).astype(BF)
        r = iota((rows, 128), 0) + start
        octant = 4 * ((r // (side * side)) % 2) + 2 * ((r // side) % 2) + r % 2
        total = None
        for o in range(8):
            part = dot(jnp.where(octant == o, pulled, jnp.zeros_like(pulled)), transfer_ref[o], NT)
            total = part if total is None else total + part
        return total

    top = 0.25 * far_ref[1152:1168] + split_down(coeffs, 16, 1, 2 * device, 0, 16)
    mid = 0.5 * far_ref[1024:1152] + split_down(top.astype(BF), 128, 2, 0, 0, 128)
    mid = mid.astype(BF)
    pl.semaphore_wait(barrier, orbs - 1)

    def copies(chunk):
        rows = pl.ds(chunk * 128, 128)
        found = []
        for away in range(1, orbs):
            found.append(
                pltpu.make_async_remote_copy(
                    src_ref=part_ref.at[rows],
                    dst_ref=other_ref.at[away - 1, rows],
                    send_sem=send.at[away - 1, chunk],
                    recv_sem=recv.at[away - 1, chunk],
                    device_id=(device, lax.rem(orb + away, orbs)),
                    device_id_type=MESH,
                )
            )
        return found

    left = iota((128, 128), 1) < 64
    for chunk in range(4):
        rows = slice(chunk * 256, (chunk + 1) * 256)
        leaf = far_ref[rows] + split_down(mid, 1024, 4, 0, chunk * 256, 256)
        leaf = leaf.astype(BF)
        coeff_ref[rows] = leaf
        wide = leaf.astype(F32)
        wide = wide + pltpu.roll(wide, 64, 1)
        packed = jnp.where(left, wide[0:128], wide[128:256])
        part_ref[chunk * 128 : (chunk + 1) * 128, :] = packed.astype(BF)
        for copy in copies(chunk):
            copy.start()
    for chunk in range(4):
        for copy in copies(chunk):
            copy.wait()
        rows = slice(chunk * 128, (chunk + 1) * 128)
        total = part_ref[rows].astype(F32)
        for away in range(1, orbs):
            total = total + other_ref[away - 1, rows].astype(F32)
        sum_ref[rows] = total.astype(BF)


def tree_down(cubes, pair, coarse, transfer, far):
    orbs = lax.axis_size("orb")
    return pl.pallas_call(
        tree_kernel,
        out_shape=[jax.ShapeDtypeStruct((1024, 128), BF), jax.ShapeDtypeStruct((512, 128), BF)],
        scratch_shapes=[
            pltpu.VMEM((2, 128, 128), BF),
            pltpu.VMEM((4, 128, 128), BF),
            pltpu.VMEM((8, 128, 128), BF),
            pltpu.VMEM((512, 128), BF),
            pltpu.VMEM((orbs - 1, 512, 128), BF),
            pltpu.SemaphoreType.DMA((orbs - 1, 4)),
            pltpu.SemaphoreType.DMA((orbs - 1, 4)),
        ],
        compiler_params=pltpu.CompilerParams(
            vmem_limit_bytes=40 << 20, collective_id=1, has_side_effects=True
        ),
        cost_estimate=pl.CostEstimate(flops=600_000_000, bytes_accessed=2 << 20, transcendentals=0),
        name="tree",
    )(cubes, pair, coarse, transfer, far)


def relax_kernel(orb_ref, near_ref, coeff_ref, near_sum_ref, coeff_sum_ref, basis_ref, out_ref, basis2_ref):
    @pl.when(pl.program_id(0) == 0)
    def _():
        spread_basis(basis_ref, basis2_ref)

    potential = near_ref[...] + dot(coeff_ref[...], basis2_ref[...])
    both = dot(coeff_sum_ref[...], basis2_ref[...])
    hartree = jnp.concatenate([both[:, :256], both[:, 256:]], axis=0) + near_sum_ref[...].astype(F32)
    for o in range(2):
        values = orb_ref[o]
        out_ref[o] = values - RELAX_STEP * (hartree - potential[:, o * 256 : (o + 1) * 256]) * values


def relax(orbitals, near, coeffs, near_sum, coeff_sum, basis):
    whole = lambda *shape: pl.BlockSpec(shape, lambda c: (0,) * len(shape))
    rows = lambda *shape: pl.BlockSpec(shape, lambda c: (c, 0))
    block = pl.BlockSpec((2, 256, 256), lambda c: (0, c, 0))
    return pl.pallas_call(
        relax_kernel,
        grid=(4,),
        in_specs=[block, rows(256, 512), rows(256, 128), rows(256, 256), rows(128, 128), whole(64, 256)],
        out_specs=block,
        out_shape=jax.ShapeDtypeStruct((2, 1024, 256), F32),
        scratch_shapes=[pltpu.VMEM((128, 512), BF)],
        compiler_params=PARAMS,
        cost_estimate=pl.CostEstimate(flops=300_000_000, bytes_accessed=8 << 20, transcendentals=0),
        name="relax",
    )(orbitals, near, coeffs, near_sum, coeff_sum, basis)


def shards(
    orbitals, near_source, far_leaf, far_mid, far_top, leaf_basis, near_table, transfer, coupling, pair_transfer,
    coarse_coupling,
):
    density, leaf, mid, top, dens_prev, dens_next, far_prev, far_next, cubes = moments(orbitals, leaf_basis, transfer)
    near, near_part = near_field(near_source, dens_prev, density, dens_next, near_table)
    near_sum = lax.psum(near_part, "orb")
    far = far_sums(far_leaf, far_mid, far_top, far_prev, leaf, mid, top, far_next, coupling)
    coeffs, coeff_sum = tree_down(cubes, pair_transfer, coarse_coupling, transfer, far)
    return relax(orbitals, near, coeffs, near_sum, coeff_sum, leaf_basis)


def solution(mesh):
    placed = (P("orb", "space", None),) + (P("space", None),) * 4 + (P(),) * 6
    return jax.shard_map(
        shards, mesh=mesh, in_specs=placed, out_specs=P("orb", "space", None), check_vma=False
    )
```

```python
import jax
import jax.numpy as jnp
from jax import lax
from jax.experimental import pallas as pl
from jax.experimental.pallas import tpu as pltpu
from jax.sharding import PartitionSpec as P

BF = jnp.bfloat16
F32 = jnp.float32
NN = (((1,), (0,)), ((), ()))
NT = (((1,), (1,)), ((), ()))
RELAX_STEP = 0.1
MESH = pl.DeviceIdType.MESH


def dot(a, b, dims=NN):
    return lax.dot_general(a, b, dims, preferred_element_type=F32)


def iota(shape, dim):
    return lax.broadcasted_iota(jnp.int32, shape, dim)


def ones_where(mask):
    return jnp.where(mask, 1.0, 0.0).astype(BF)


def one_hot(column, rows, width):
    return ones_where(iota((rows, width), 1) == column)


def octant_picker(parents, half, width):
    row, col = iota((8 * parents, width), 0), iota((8 * parents, width), 1)
    octant, b = row // parents, row % parents
    z, y, x = b // (half * half), (b // half) % half, b % half
    dz, dy, dx = octant // 4, (octant // 2) % 2, octant % 2
    side = 2 * half
    child = ((2 * z + dz) * side + 2 * y + dy) * side + 2 * x + dx
    return ones_where(child == col)


def merge_up(picked, parents, transfer_ref):
    total = None
    for octant in range(8):
        part = dot(picked[octant * parents : (octant + 1) * parents], transfer_ref[octant])
        total = part if total is None else total + part
    return total.astype(BF)


def spread(matrix):
    zero = jnp.zeros_like(matrix)
    top = jnp.concatenate([matrix, zero], axis=1)
    return jnp.concatenate([top, jnp.concatenate([zero, matrix], axis=1)], axis=0)


def spread_basis(basis_ref, basis2_ref):
    basis2_ref[...] = jnp.zeros((128, 512), BF)
    basis2_ref[0:64, 0:256] = basis_ref[...]
    basis2_ref[64:128, 256:512] = basis_ref[...]


def step_kernel(
    orb_hbm, near_list, leaf_list, mid_list, top_list, basis_ref, table_hbm, transfer_in, coupling_hbm, pair_in, coarse_in,
    out_hbm,
    orb_ref, table_ref, coupling_ref, dens_ref, leaf_ref, mid_ref, top_ref, cube_ref, basis2_ref, transfer_ref, pair_ref,
    coarse_ref, weight_ref, hot_ref, near_pick, far_pick, near_ref, near_part, near_other, coeff_ref, coeff_part, coeff_other,
    load_sem, out_sem, halo_send, halo_recv, cube_send, cube_recv, near_send, near_recv, coeff_send, coeff_recv,
):
    me, orb = lax.axis_index("space"), lax.axis_index("orb")
    count, orbs = lax.axis_size("space"), lax.axis_size("orb")
    after, before = lax.rem(me + 1, count), lax.rem(me + count - 1, count)
    barrier = pltpu.get_barrier_semaphore()

    def greet(i, _):
        other = lax.rem(me + i, count)
        pl.semaphore_signal(barrier, inc=1, device_id=(other, orb), device_id_type=MESH)
        return 0

    lax.fori_loop(1, count, greet, 0)
    for away in range(1, orbs):
        other = lax.rem(orb + away, orbs)
        pl.semaphore_signal(barrier, inc=1, device_id=(me, other), device_id_type=MESH)

    def rows_of(c, size):
        return pl.ds(pl.multiple_of(c * size, size), size)

    def load_orbitals(c):
        rows = rows_of(c, 256)
        return pltpu.make_async_copy(orb_hbm.at[:, rows], orb_ref.at[:, rows], load_sem.at[c])

    load_table = pltpu.make_async_copy(table_hbm, table_ref, load_sem.at[4])
    load_coupling = pltpu.make_async_copy(coupling_hbm, coupling_ref, load_sem.at[5])
    for c in range(4):
        load_orbitals(c).start()
    load_table.start()
    load_coupling.start()

    spread_basis(basis_ref, basis2_ref)
    for given, kept in ((pair_in, pair_ref), (coarse_in, coarse_ref), (transfer_in, transfer_ref)):
        for i in range(given.shape[0]):
            kept[i] = spread(given[i])
    mid_ref[224:256, :] = jnp.zeros((32, 128), BF)
    top_ref[48:128, :] = jnp.zeros((80, 128), BF)

    def moments_chunk(c, _):
        load_orbitals(c).wait()
        rows = rows_of(c, 256)
        inner = pl.ds(pl.multiple_of(64 + c * 256, 64), 256)
        for o in range(2):
            values = orb_ref[o, rows, :]
            dens_ref[inner, o * 256 : (o + 1) * 256] = (values * values).astype(BF)
        leaf = dot(dens_ref[inner, :], basis2_ref[...], NT).astype(BF)
        leaf_ref[pl.ds(pl.multiple_of(192 + c * 256, 64), 256), :] = leaf
        picked = dot(octant_picker(32, 4, 256), leaf).astype(BF)
        mid_ref[pl.ds(pl.multiple_of(48 + c * 32, 16), 32), :] = merge_up(picked, 32, transfer_ref)
        return 0

    lax.fori_loop(0, 4, moments_chunk, 0)
    pl.semaphore_wait(barrier, count - 1 + orbs - 1)

    def halo(number, ref, head, tail, rows, ahead):
        source, target, device = (tail, 0, after) if ahead else (head, tail + rows, before)
        return pltpu.make_async_remote_copy(
            src_ref=ref.at[pl.ds(source, rows)],
            dst_ref=ref.at[pl.ds(target, rows)],
            send_sem=halo_send.at[number],
            recv_sem=halo_recv.at[number],
            device_id=(device, orb),
            device_id_type=MESH,
        )

    halos = []
    for ref, head, tail, rows in (
        (dens_ref, 64, 1024, 64),
        (leaf_ref, 192, 1024, 192),
        (mid_ref, 48, 128, 48),
        (top_ref, 16, 16, 16),
    ):
        for ahead in (False, True):
            halos.append(halo(len(halos), ref, head, tail, rows, ahead))
    for copy in halos[0:6]:
        copy.start()
    top = merge_up(dot(octant_picker(16, 2, 128), mid_ref[48:176, :]).astype(BF), 16, transfer_ref)
    top_ref[16:32, :] = top
    for copy in halos[6:8]:
        copy.start()
    cube_ref[rows_of(me, 16), :] = merge_up(
        dot(octant_picker(16, 1, 16), top).astype(BF), 16, transfer_ref
    )

    def cube_copy(other, owner):
        block = cube_ref.at[rows_of(owner, 16)]
        return pltpu.make_async_remote_copy(
            src_ref=block,
            dst_ref=block,
            send_sem=cube_send.at[other],
            recv_sem=cube_recv.at[owner],
            device_id=(other, orb),
            device_id_type=MESH,
        )

    def send_cube(i, _):
        cube_copy(lax.rem(me + i, count), me).start()
        return 0

    lax.fori_loop(1, count, send_cube, 0)

    def to_orbs(part, landing, send, recv, c, size):
        rows = rows_of(c, size)
        return [
            pltpu.make_async_remote_copy(
                src_ref=part.at[rows],
                dst_ref=landing.at[away - 1, rows],
                send_sem=send.at[away - 1, c],
                recv_sem=recv.at[away - 1, c],
                device_id=(me, lax.rem(orb + away, orbs)),
                device_id_type=MESH,
            )
            for away in range(1, orbs)
        ]

    load_table.wait()

    def near_chunk(i, _):
        c = lax.rem(i + 1, 4)

        @pl.when(i == 2)
        def _():
            for copy in halos[0:2]:
                copy.wait()

        for part in range(2):
            base = pl.multiple_of(c * 256 + part * 128, 128)
            place = (near_list[:, pl.ds(base, 128)].T + (64 + 128 * part)) & 255
            for k in range(27):
                hot_ref[k * 128 : (k + 1) * 128, :] = one_hot(place[:, k : k + 1], 128, 256)
            for o in range(2):
                source = dens_ref[pl.ds(base, 256), o * 256 : (o + 1) * 256]
                at = o * 256 + part * 128
                for first in range(0, 27, 9):
                    picked = dot(hot_ref[first * 128 : (first + 9) * 128, :], source).astype(BF)
                    for k in range(9):
                        near_pick[at : at + 128, (first + k) * 256 : (first + k + 1) * 256] = picked[
                            k * 128 : (k + 1) * 128
                        ]
        total = None
        for k in range(27):
            part = dot(near_pick[:, k * 256 : (k + 1) * 256], table_ref[k], NT)
            total = part if total is None else total + part
        rows = rows_of(c, 256)
        near_ref[rows, 0:256] = total[:256]
        near_ref[rows, 256:512] = total[256:]
        near_part[rows, :] = (total[:256] + total[256:]).astype(BF)
        for copy in to_orbs(near_part, near_other, near_send, near_recv, c, 256):
            copy.start()
        return 0

    lax.fori_loop(0, 4, near_chunk, 0)

    load_coupling.wait()
    for k in range(108):
        weight_ref[:, k * 128 : (k + 1) * 128] = spread(coupling_ref[k])
    for copy in halos[2:8]:
        copy.wait()

    def pick(place, rows, at, table):
        width = table.shape[0]
        for k in range(108):
            hot_ref[k * rows : (k + 1) * rows, :width] = one_hot(place[:, k : k + 1], rows, width)
        for first in range(0, 108, 12):
            picked = dot(hot_ref[first * rows : (first + 12) * rows, :width], table).astype(BF)
            for k in range(12):
                far_pick[at : at + rows, (first + k) * 128 : (first + k + 1) * 128] = picked[
                    k * rows : (k + 1) * rows
                ]

    mid_place = mid_list[...].T - (me * 128 - 48)
    pick(mid_place[0:64], 64, 0, mid_ref[...])
    pick(mid_place[64:128], 64, 64, mid_ref[...])
    pick(top_list[...].T - (me * 16 - 16), 16, 128, top_ref[...])
    far = dot(far_pick[0:144, :], weight_ref[...], NT)

    def wait_cube(i, _):
        other = lax.rem(me + i, count)
        cube_copy(other, me).wait_send()
        cube_copy(other, other).wait_recv()
        return 0

    lax.fori_loop(1, count, wait_cube, 0)
    row, col = iota((64, cube_ref.shape[0]), 0), iota((64, cube_ref.shape[0]), 1)
    cubes = dot(ones_where(col == 16 * (row // 2) + row % 2), cube_ref[...]).astype(BF)
    row, col = iota((64, 64), 0), iota((64, 64), 1)
    child = [ones_where(col == 2 * row + p) for p in range(2)]
    mother = [ones_where((col == row // 2) & (row % 2 == p)) for p in range(2)]
    shift = [
        ones_where((col == row - 3) & (row % 2 == 1)),
        ones_where(col == row - 2),
        ones_where(col == row + 2),
        ones_where((col == row + 3) & (row % 2 == 0)),
    ]
    levels = [cubes]
    for _ in range(6):
        total = None
        for p in range(2):
            part = dot(dot(child[p], levels[-1]).astype(BF), pair_ref[p])
            total = part if total is None else total + part
        levels.append(total.astype(BF))
    coeffs = None
    for depth in range(6, -1, -1):
        total = None
        for w in range(4):
            part = dot(dot(shift[w], levels[depth]).astype(BF), coarse_ref[w], NT)
            total = part if total is None else total + part
        total = total * (0.5 ** (3 + depth))
        if coeffs is not None:
            for p in range(2):
                total = total + dot(dot(mother[p], coeffs).astype(BF), pair_ref[p], NT)
        coeffs = total.astype(BF)

    def split_down(coeffs, half, first, start, rows):
        parents = coeffs.shape[0]
        side = 2 * half
        row, col = iota((rows, parents), 0) + start, iota((rows, parents), 1)
        z, y, x = row // (side * side), (row // side) % side, row % side
        parent = ((z // 2) * half + y // 2) * half + x // 2 + first
        pulled = dot(ones_where(col == parent), coeffs).astype(BF)
        r = iota((rows, 128), 0) + start
        octant = 4 * ((r // (side * side)) % 2) + 2 * ((r // side) % 2) + r % 2
        total = None
        for o in range(8):
            part = dot(jnp.where(octant == o, pulled, jnp.zeros_like(pulled)), transfer_ref[o], NT)
            total = part if total is None else total + part
        return total

    top = 0.25 * far[128:144] + split_down(coeffs, 1, 2 * me, 0, 16)
    mid = 0.5 * far[0:128] + split_down(top.astype(BF), 2, 0, 0, 128)
    mid_ref[0:128, :] = mid.astype(BF)

    def leaf_chunk(c, _):
        for half in range(2):
            start = pl.multiple_of(c * 256 + half * 128, 128)
            offset = (leaf_list[:, pl.ds(start, 128)].T - c * 256 - half * 128 + 192) & 1023
            for layer in range(2):
                base = pl.multiple_of(start + layer * 64, 64)
                place = (offset[layer * 64 : (layer + 1) * 64] - 64 * layer) & 1023
                place = jnp.where(place < 128, place, place - 192)
                table = jnp.concatenate(
                    [leaf_ref[pl.ds(base, 128), :], leaf_ref[pl.ds(base + 320, 128), :]], axis=0
                )
                pick(place, 64, half * 128 + layer * 64, table)
        leaf = dot(far_pick[...], weight_ref[...], NT) + split_down(mid_ref[0:128, :], 4, 0, c * 256, 256)
        leaf = leaf.astype(BF)
        coeff_ref[rows_of(c, 256), :] = leaf
        wide = leaf.astype(F32)
        wide = wide + pltpu.roll(wide, 64, 1)
        packed = jnp.where(iota((128, 128), 1) < 64, wide[0:128], wide[128:256])
        coeff_part[rows_of(c, 128), :] = packed.astype(BF)
        for copy in to_orbs(coeff_part, coeff_other, coeff_send, coeff_recv, c, 128):
            copy.start()
        return 0

    lax.fori_loop(0, 4, leaf_chunk, 0)

    def store(c):
        rows = rows_of(c, 256)
        return pltpu.make_async_copy(orb_ref.at[:, rows], out_hbm.at[:, rows], out_sem.at[c])

    def relax_chunk(c, _):
        for copy in to_orbs(near_part, near_other, near_send, near_recv, c, 256):
            copy.wait()
        for copy in to_orbs(coeff_part, coeff_other, coeff_send, coeff_recv, c, 128):
            copy.wait()
        rows, packed_rows = rows_of(c, 256), rows_of(c, 128)
        packed = coeff_part[packed_rows, :].astype(F32)
        hartree = near_part[rows, :].astype(F32)
        for away in range(orbs - 1):
            packed = packed + coeff_other[away, packed_rows, :].astype(F32)
            hartree = hartree + near_other[away, rows, :].astype(F32)
        both = dot(packed.astype(BF), basis2_ref[...])
        hartree = hartree + jnp.concatenate([both[:, :256], both[:, 256:]], axis=0)
        potential = near_ref[rows, :] + dot(coeff_ref[rows, :], basis2_ref[...])
        for o in range(2):
            values = orb_ref[o, rows, :]
            orb_ref[o, rows, :] = values - RELAX_STEP * (hartree - potential[:, o * 256 : (o + 1) * 256]) * values
        store(c).start()
        return 0

    lax.fori_loop(0, 4, relax_chunk, 0)
    for c in range(4):
        store(c).wait()


def shards(
    orbitals, near_source, far_leaf, far_mid, far_top, leaf_basis, near_table, transfer, coupling, pair_transfer,
    coarse_coupling,
):
    count, orbs = lax.axis_size("space"), lax.axis_size("orb")
    near_by, here = pl.BlockSpec(memory_space=pl.ANY), pl.BlockSpec(memory_space=pltpu.VMEM)
    return pl.pallas_call(
        step_kernel,
        in_specs=[near_by, here, here, here, here, here, near_by, here, near_by, here, here],
        out_specs=near_by,
        out_shape=jax.ShapeDtypeStruct((2, 1024, 256), F32),
        scratch_shapes=[
            pltpu.VMEM((2, 1024, 256), F32),
            pltpu.VMEM((27, 256, 256), BF),
            pltpu.VMEM((108, 64, 64), BF),
            pltpu.VMEM((1152, 512), BF),
            pltpu.VMEM((1408, 128), BF),
            pltpu.VMEM((256, 128), BF),
            pltpu.VMEM((128, 128), BF),
            pltpu.VMEM((count * 16, 128), BF),
            pltpu.VMEM((128, 512), BF),
            pltpu.VMEM((8, 128, 128), BF),
            pltpu.VMEM((2, 128, 128), BF),
            pltpu.VMEM((4, 128, 128), BF),
            pltpu.VMEM((128, 108 * 128), BF),
            pltpu.VMEM((108 * 64, 256), BF),
            pltpu.VMEM((512, 27 * 256), BF),
            pltpu.VMEM((256, 108 * 128), BF),
            pltpu.VMEM((1024, 512), F32),
            pltpu.VMEM((1024, 256), BF),
            pltpu.VMEM((orbs - 1, 1024, 256), BF),
            pltpu.VMEM((1024, 128), BF),
            pltpu.VMEM((512, 128), BF),
            pltpu.VMEM((orbs - 1, 512, 128), BF),
            pltpu.SemaphoreType.DMA((6,)),
            pltpu.SemaphoreType.DMA((4,)),
            pltpu.SemaphoreType.DMA((8,)),
            pltpu.SemaphoreType.DMA((8,)),
            pltpu.SemaphoreType.DMA((count,)),
            pltpu.SemaphoreType.DMA((count,)),
            pltpu.SemaphoreType.DMA((orbs - 1, 4)),
            pltpu.SemaphoreType.DMA((orbs - 1, 4)),
            pltpu.SemaphoreType.DMA((orbs - 1, 4)),
            pltpu.SemaphoreType.DMA((orbs - 1, 4)),
        ],
        compiler_params=pltpu.CompilerParams(vmem_limit_bytes=52 << 20, collective_id=0, has_side_effects=True),
        cost_estimate=pl.CostEstimate(flops=36_000_000_000, bytes_accessed=12 << 20, transcendentals=0),
        name="step",
    )(
        orbitals, near_source.T, far_leaf.T, far_mid.T, far_top.T, leaf_basis, near_table, transfer, coupling,
        pair_transfer, coarse_coupling,
    )


def solution(mesh):
    placed = (P("orb", "space", None),) + (P("space", None),) * 4 + (P(),) * 6
    return jax.shard_map(
        shards, mesh=mesh, in_specs=placed, out_specs=P("orb", "space", None), check_vma=False
    )
```

```python
import jax
import jax.numpy as jnp
from jax import lax
from jax.experimental import pallas as pl
from jax.experimental.pallas import tpu as pltpu
from jax.sharding import PartitionSpec as P

BF = jnp.bfloat16
F32 = jnp.float32
NN = (((1,), (0,)), ((), ()))
NT = (((1,), (1,)), ((), ()))
RELAX_STEP = 0.1
MESH = pl.DeviceIdType.MESH


def dot(a, b, dims=NN):
    return lax.dot_general(a, b, dims, preferred_element_type=F32)


def iota(shape, dim):
    return lax.broadcasted_iota(jnp.int32, shape, dim)


def ones_where(mask):
    return jnp.where(mask, 1.0, 0.0).astype(BF)


def one_hot(places, first, number, rows, width):
    lane = iota((rows, width), 1).astype(BF)
    found = [
        jnp.where(lane == places[:, k : k + 1], BF(1), BF(0)) for k in range(first, first + number)
    ]
    return jnp.concatenate(found, axis=0)


def as_place(numbers):
    return numbers.astype(F32).astype(BF)


def octant_picker(parents, half, width):
    row, col = iota((8 * parents, width), 0), iota((8 * parents, width), 1)
    octant, b = row // parents, row % parents
    z, y, x = b // (half * half), (b // half) % half, b % half
    dz, dy, dx = octant // 4, (octant // 2) % 2, octant % 2
    side = 2 * half
    child = ((2 * z + dz) * side + 2 * y + dy) * side + 2 * x + dx
    return ones_where(child == col)


def merge_up(picked, parents, transfer_ref):
    total = None
    for octant in range(8):
        part = dot(picked[octant * parents : (octant + 1) * parents], transfer_ref[octant])
        total = part if total is None else total + part
    return total.astype(BF)


def spread(matrix):
    zero = jnp.zeros_like(matrix)
    top = jnp.concatenate([matrix, zero], axis=1)
    return jnp.concatenate([top, jnp.concatenate([zero, matrix], axis=1)], axis=0)


def spread_basis(basis_ref, basis2_ref):
    basis2_ref[...] = jnp.zeros((128, 512), BF)
    basis2_ref[0:64, 0:256] = basis_ref[...]
    basis2_ref[64:128, 256:512] = basis_ref[...]


def step_kernel(
    orb_hbm, near_list, leaf_list, mid_list, top_list, basis_ref, table_hbm, transfer_in, coupling_hbm, pair_in, coarse_in,
    out_ref,
    orb_ref, table_ref, coupling_ref, dens_ref, leaf_ref, mid_ref, top_ref, cube_ref, basis2_ref, transfer_ref, pair_ref,
    coarse_ref, weight_ref, near_pick, far_pick, near_ref, near_part, near_other, coeff_ref, coeff_part, coeff_other,
    load_sem, halo_send, halo_recv, cube_send, cube_recv, near_send, near_recv, coeff_send, coeff_recv,
):
    me, orb = lax.axis_index("space"), lax.axis_index("orb")
    count, orbs = lax.axis_size("space"), lax.axis_size("orb")
    after, before = lax.rem(me + 1, count), lax.rem(me + count - 1, count)
    barrier = pltpu.get_barrier_semaphore()

    def greet(i, _):
        other = lax.rem(me + i, count)
        pl.semaphore_signal(barrier, inc=1, device_id=(other, orb), device_id_type=MESH)
        return 0

    lax.fori_loop(1, count, greet, 0)
    for away in range(1, orbs):
        other = lax.rem(orb + away, orbs)
        pl.semaphore_signal(barrier, inc=1, device_id=(me, other), device_id_type=MESH)

    def rows_of(c, size):
        return pl.ds(pl.multiple_of(c * size, size), size)

    def load_orbitals(c):
        rows = rows_of(c, 256)
        return pltpu.make_async_copy(orb_hbm.at[:, rows], orb_ref.at[:, rows], load_sem.at[c])

    load_table = pltpu.make_async_copy(table_hbm, table_ref, load_sem.at[4])
    load_coupling = pltpu.make_async_copy(coupling_hbm, coupling_ref, load_sem.at[5])
    for c in range(4):
        load_orbitals(c).start()
    load_table.start()
    load_coupling.start()

    spread_basis(basis_ref, basis2_ref)
    for given, kept in ((pair_in, pair_ref), (coarse_in, coarse_ref), (transfer_in, transfer_ref)):
        for i in range(given.shape[0]):
            kept[i] = spread(given[i])
    mid_ref[224:256, :] = jnp.zeros((32, 128), BF)
    top_ref[48:128, :] = jnp.zeros((80, 128), BF)

    def moments_chunk(c, _):
        load_orbitals(c).wait()
        rows = rows_of(c, 256)
        inner = pl.ds(pl.multiple_of(64 + c * 256, 64), 256)
        for o in range(2):
            values = orb_ref[o, rows, :]
            dens_ref[inner, o * 256 : (o + 1) * 256] = (values * values).astype(BF)
        leaf = dot(dens_ref[inner, :], basis2_ref[...], NT).astype(BF)
        leaf_ref[pl.ds(pl.multiple_of(192 + c * 256, 64), 256), :] = leaf
        picked = dot(octant_picker(32, 4, 256), leaf).astype(BF)
        mid_ref[pl.ds(pl.multiple_of(48 + c * 32, 16), 32), :] = merge_up(picked, 32, transfer_ref)
        return 0

    lax.fori_loop(0, 4, moments_chunk, 0)
    pl.semaphore_wait(barrier, count - 1 + orbs - 1)

    def halo(number, ref, head, tail, rows, ahead):
        source, target, device = (tail, 0, after) if ahead else (head, tail + rows, before)
        return pltpu.make_async_remote_copy(
            src_ref=ref.at[pl.ds(source, rows)],
            dst_ref=ref.at[pl.ds(target, rows)],
            send_sem=halo_send.at[number],
            recv_sem=halo_recv.at[number],
            device_id=(device, orb),
            device_id_type=MESH,
        )

    halos = []
    for ref, head, tail, rows in (
        (dens_ref, 64, 1024, 64),
        (leaf_ref, 192, 1024, 192),
        (mid_ref, 48, 128, 48),
        (top_ref, 16, 16, 16),
    ):
        for ahead in (False, True):
            halos.append(halo(len(halos), ref, head, tail, rows, ahead))
    for copy in halos[0:6]:
        copy.start()
    top = merge_up(dot(octant_picker(16, 2, 128), mid_ref[48:176, :]).astype(BF), 16, transfer_ref)
    top_ref[16:32, :] = top
    for copy in halos[6:8]:
        copy.start()
    cube_ref[rows_of(me, 16), :] = merge_up(
        dot(octant_picker(16, 1, 16), top).astype(BF), 16, transfer_ref
    )

    def cube_copy(other, owner):
        block = cube_ref.at[rows_of(owner, 16)]
        return pltpu.make_async_remote_copy(
            src_ref=block,
            dst_ref=block,
            send_sem=cube_send.at[other],
            recv_sem=cube_recv.at[owner],
            device_id=(other, orb),
            device_id_type=MESH,
        )

    def send_cube(i, _):
        cube_copy(lax.rem(me + i, count), me).start()
        return 0

    lax.fori_loop(1, count, send_cube, 0)

    def to_orbs(part, landing, send, recv, c, size):
        rows = rows_of(c, size)
        return [
            pltpu.make_async_remote_copy(
                src_ref=part.at[rows],
                dst_ref=landing.at[away - 1, rows],
                send_sem=send.at[away - 1, c],
                recv_sem=recv.at[away - 1, c],
                device_id=(me, lax.rem(orb + away, orbs)),
                device_id_type=MESH,
            )
            for away in range(1, orbs)
        ]

    load_table.wait()

    def near_chunk(i, _):
        c = lax.rem(i + 1, 4)

        @pl.when(i == 2)
        def _():
            for copy in halos[0:2]:
                copy.wait()

        for part in range(2):
            base = pl.multiple_of(c * 256 + part * 128, 128)
            place = as_place((near_list[:, pl.ds(base, 128)].T + (64 + 128 * part)) & 255)
            for first in range(0, 27, 3):
                hot = one_hot(place, first, 3, 128, 256)
                for o in range(2):
                    source = dens_ref[pl.ds(base, 256), o * 256 : (o + 1) * 256]
                    at = o * 256 + part * 128
                    picked = dot(hot, source).astype(BF)
                    for k in range(3):
                        near_pick[at : at + 128, (first + k) * 256 : (first + k + 1) * 256] = picked[
                            k * 128 : (k + 1) * 128
                        ]
        total = None
        for k in range(27):
            part = dot(near_pick[:, k * 256 : (k + 1) * 256], table_ref[k], NT)
            total = part if total is None else total + part
        rows = rows_of(c, 256)
        near_ref[rows, 0:256] = total[:256]
        near_ref[rows, 256:512] = total[256:]
        near_part[rows, :] = (total[:256] + total[256:]).astype(BF)
        for copy in to_orbs(near_part, near_other, near_send, near_recv, c, 256):
            copy.start()
        return 0

    lax.fori_loop(0, 4, near_chunk, 0)

    load_coupling.wait()
    for k in range(108):
        weight_ref[:, k * 128 : (k + 1) * 128] = spread(coupling_ref[k])
    for copy in halos[2:8]:
        copy.wait()

    def pick(place, rows, at, table):
        number = 128 // rows
        place = as_place(place)
        for first in range(0, 108, number):
            number = min(number, 108 - first)
            hot = one_hot(place, first, number, rows, table.shape[0])
            picked = dot(hot, table).astype(BF)
            for k in range(number):
                far_pick[at : at + rows, (first + k) * 128 : (first + k + 1) * 128] = picked[
                    k * rows : (k + 1) * rows
                ]

    mid_place = mid_list[...].T - (me * 128 - 48)
    pick(mid_place[0:64], 64, 0, mid_ref[...])
    pick(mid_place[64:128], 64, 64, mid_ref[...])
    pick(top_list[...].T - (me * 16 - 16), 16, 128, top_ref[...])
    far = dot(far_pick[0:144, :], weight_ref[...], NT)

    def wait_cube(i, _):
        other = lax.rem(me + i, count)
        cube_copy(other, me).wait_send()
        cube_copy(other, other).wait_recv()
        return 0

    lax.fori_loop(1, count, wait_cube, 0)
    row, col = iota((64, cube_ref.shape[0]), 0), iota((64, cube_ref.shape[0]), 1)
    cubes = dot(ones_where(col == 16 * (row // 2) + row % 2), cube_ref[...]).astype(BF)
    row, col = iota((64, 64), 0), iota((64, 64), 1)
    child = [ones_where(col == 2 * row + p) for p in range(2)]
    mother = [ones_where((col == row // 2) & (row % 2 == p)) for p in range(2)]
    shift = [
        ones_where((col == row - 3) & (row % 2 == 1)),
        ones_where(col == row - 2),
        ones_where(col == row + 2),
        ones_where((col == row + 3) & (row % 2 == 0)),
    ]
    levels = [cubes]
    for _ in range(6):
        total = None
        for p in range(2):
            part = dot(dot(child[p], levels[-1]).astype(BF), pair_ref[p])
            total = part if total is None else total + part
        levels.append(total.astype(BF))
    coeffs = None
    for depth in range(6, -1, -1):
        total = None
        for w in range(4):
            part = dot(dot(shift[w], levels[depth]).astype(BF), coarse_ref[w], NT)
            total = part if total is None else total + part
        total = total * (0.5 ** (3 + depth))
        if coeffs is not None:
            for p in range(2):
                total = total + dot(dot(mother[p], coeffs).astype(BF), pair_ref[p], NT)
        coeffs = total.astype(BF)

    def split_down(coeffs, half, first, start, rows):
        parents = coeffs.shape[0]
        side = 2 * half
        row, col = iota((rows, parents), 0) + start, iota((rows, parents), 1)
        z, y, x = row // (side * side), (row // side) % side, row % side
        parent = ((z // 2) * half + y // 2) * half + x // 2 + first
        pulled = dot(ones_where(col == parent), coeffs).astype(BF)
        r = iota((rows, 128), 0) + start
        octant = 4 * ((r // (side * side)) % 2) + 2 * ((r // side) % 2) + r % 2
        total = None
        for o in range(8):
            part = dot(jnp.where(octant == o, pulled, jnp.zeros_like(pulled)), transfer_ref[o], NT)
            total = part if total is None else total + part
        return total

    top = 0.25 * far[128:144] + split_down(coeffs, 1, 2 * me, 0, 16)
    mid = 0.5 * far[0:128] + split_down(top.astype(BF), 2, 0, 0, 128)
    mid_ref[0:128, :] = mid.astype(BF)

    def leaf_chunk(c, _):
        for half in range(2):
            start = pl.multiple_of(c * 256 + half * 128, 128)
            offset = (leaf_list[:, pl.ds(start, 128)].T - c * 256 - half * 128 + 192) & 1023
            for layer in range(2):
                base = pl.multiple_of(start + layer * 64, 64)
                place = (offset[layer * 64 : (layer + 1) * 64] - 64 * layer) & 1023
                place = jnp.where(place < 128, place, place - 192)
                table = jnp.concatenate(
                    [leaf_ref[pl.ds(base, 128), :], leaf_ref[pl.ds(base + 320, 128), :]], axis=0
                )
                pick(place, 64, half * 128 + layer * 64, table)
        leaf = dot(far_pick[...], weight_ref[...], NT) + split_down(mid_ref[0:128, :], 4, 0, c * 256, 256)
        leaf = leaf.astype(BF)
        coeff_ref[rows_of(c, 256), :] = leaf
        wide = leaf.astype(F32)
        wide = wide + pltpu.roll(wide, 64, 1)
        packed = jnp.where(iota((128, 128), 1) < 64, wide[0:128], wide[128:256])
        coeff_part[rows_of(c, 128), :] = packed.astype(BF)
        for copy in to_orbs(coeff_part, coeff_other, coeff_send, coeff_recv, c, 128):
            copy.start()
        return 0

    lax.fori_loop(0, 4, leaf_chunk, 0)

    def change_chunk(c, _):
        for copy in to_orbs(near_part, near_other, near_send, near_recv, c, 256):
            copy.wait()
        for copy in to_orbs(coeff_part, coeff_other, coeff_send, coeff_recv, c, 128):
            copy.wait()
        rows, packed_rows = rows_of(c, 256), rows_of(c, 128)
        packed = coeff_part[packed_rows, :].astype(F32)
        hartree = near_part[rows, :].astype(F32)
        for away in range(orbs - 1):
            packed = packed + coeff_other[away, packed_rows, :].astype(F32)
            hartree = hartree + near_other[away, rows, :].astype(F32)
        both = dot(packed.astype(BF), basis2_ref[...])
        hartree = hartree + jnp.concatenate([both[:, :256], both[:, 256:]], axis=0)
        potential = near_ref[rows, :] + dot(coeff_ref[rows, :], basis2_ref[...])
        for o in range(2):
            out_ref[o, rows, :] = hartree - potential[:, o * 256 : (o + 1) * 256]
        return 0

    lax.fori_loop(0, 4, change_chunk, 0)


def shards(
    orbitals, near_source, far_leaf, far_mid, far_top, leaf_basis, near_table, transfer, coupling, pair_transfer,
    coarse_coupling,
):
    count, orbs = lax.axis_size("space"), lax.axis_size("orb")
    near_by, here = pl.BlockSpec(memory_space=pl.ANY), pl.BlockSpec(memory_space=pltpu.VMEM)
    change = pl.pallas_call(
        step_kernel,
        in_specs=[near_by, here, here, here, here, here, near_by, here, near_by, here, here],
        out_specs=here,
        out_shape=jax.ShapeDtypeStruct((2, 1024, 256), F32),
        scratch_shapes=[
            pltpu.VMEM((2, 1024, 256), F32),
            pltpu.VMEM((27, 256, 256), BF),
            pltpu.VMEM((108, 64, 64), BF),
            pltpu.VMEM((1152, 512), BF),
            pltpu.VMEM((1408, 128), BF),
            pltpu.VMEM((256, 128), BF),
            pltpu.VMEM((128, 128), BF),
            pltpu.VMEM((count * 16, 128), BF),
            pltpu.VMEM((128, 512), BF),
            pltpu.VMEM((8, 128, 128), BF),
            pltpu.VMEM((2, 128, 128), BF),
            pltpu.VMEM((4, 128, 128), BF),
            pltpu.VMEM((128, 108 * 128), BF),
            pltpu.VMEM((512, 27 * 256), BF),
            pltpu.VMEM((256, 108 * 128), BF),
            pltpu.VMEM((1024, 512), F32),
            pltpu.VMEM((1024, 256), BF),
            pltpu.VMEM((orbs - 1, 1024, 256), BF),
            pltpu.VMEM((1024, 128), BF),
            pltpu.VMEM((512, 128), BF),
            pltpu.VMEM((orbs - 1, 512, 128), BF),
            pltpu.SemaphoreType.DMA((6,)),
            pltpu.SemaphoreType.DMA((8,)),
            pltpu.SemaphoreType.DMA((8,)),
            pltpu.SemaphoreType.DMA((count,)),
            pltpu.SemaphoreType.DMA((count,)),
            pltpu.SemaphoreType.DMA((orbs - 1, 4)),
            pltpu.SemaphoreType.DMA((orbs - 1, 4)),
            pltpu.SemaphoreType.DMA((orbs - 1, 4)),
            pltpu.SemaphoreType.DMA((orbs - 1, 4)),
        ],
        compiler_params=pltpu.CompilerParams(vmem_limit_bytes=48 << 20, collective_id=0, has_side_effects=True),
        cost_estimate=pl.CostEstimate(flops=36_000_000_000, bytes_accessed=12 << 20, transcendentals=0),
        name="step",
    )(
        orbitals, near_source.T, far_leaf.T, far_mid.T, far_top.T, leaf_basis, near_table, transfer, coupling,
        pair_transfer, coarse_coupling,
    )
    return orbitals - RELAX_STEP * change * orbitals


def solution(mesh):
    placed = (P("orb", "space", None),) + (P("space", None),) * 4 + (P(),) * 6
    return jax.shard_map(
        shards, mesh=mesh, in_specs=placed, out_specs=P("orb", "space", None), check_vma=False
    )
```

```python
import jax
import jax.numpy as jnp
from jax import lax
from jax.experimental import pallas as pl
from jax.experimental.pallas import tpu as pltpu
from jax.sharding import PartitionSpec as P

BF = jnp.bfloat16
F32 = jnp.float32
NN = (((1,), (0,)), ((), ()))
NT = (((1,), (1,)), ((), ()))
RELAX_STEP = 0.1
MESH = pl.DeviceIdType.MESH


def dot(a, b, dims=NN):
    return lax.dot_general(a, b, dims, preferred_element_type=F32)


def iota(shape, dim):
    return lax.broadcasted_iota(jnp.int32, shape, dim)


def ones_where(mask):
    return jnp.where(mask, 1.0, 0.0).astype(BF)


def one_hot(places, first, number, rows, width):
    lane = iota((rows, width), 1).astype(BF)
    found = [
        jnp.where(lane == places[:, k : k + 1], BF(1), BF(0)) for k in range(first, first + number)
    ]
    return jnp.concatenate(found, axis=0)


def as_place(numbers):
    return numbers.astype(F32).astype(BF)


def octant_picker(parents, half, width):
    row, col = iota((8 * parents, width), 0), iota((8 * parents, width), 1)
    octant, b = row // parents, row % parents
    z, y, x = b // (half * half), (b // half) % half, b % half
    dz, dy, dx = octant // 4, (octant // 2) % 2, octant % 2
    side = 2 * half
    child = ((2 * z + dz) * side + 2 * y + dy) * side + 2 * x + dx
    return ones_where(child == col)


def merge_up(picked, parents, transfer_ref):
    total = None
    for octant in range(8):
        part = dot(picked[octant * parents : (octant + 1) * parents], transfer_ref[octant])
        total = part if total is None else total + part
    return total.astype(BF)


def spread(matrix):
    zero = jnp.zeros_like(matrix)
    top = jnp.concatenate([matrix, zero], axis=1)
    return jnp.concatenate([top, jnp.concatenate([zero, matrix], axis=1)], axis=0)


def spread_basis(basis_ref, basis2_ref):
    basis2_ref[...] = jnp.zeros((128, 512), BF)
    basis2_ref[0:64, 0:256] = basis_ref[...]
    basis2_ref[64:128, 256:512] = basis_ref[...]


def step_kernel(
    orb_hbm, near_list, leaf_list, mid_list, top_list, basis_ref, table_hbm, transfer_in, coupling_hbm, pair_in, coarse_in,
    out_ref,
    orb_ref, table_ref, coupling_ref, turned_ref, dens_ref, leaf_ref, mid_ref, top_ref, cube_ref, basis2_ref, transfer_ref, pair_ref,
    coarse_ref, weight_ref, near_pick, far_pick, near_ref, near_part, near_other, coeff_ref, coeff_part, coeff_other,
    load_sem, halo_send, halo_recv, cube_send, cube_recv, near_send, near_recv, coeff_send, coeff_recv,
):
    me, orb = lax.axis_index("space"), lax.axis_index("orb")
    count, orbs = lax.axis_size("space"), lax.axis_size("orb")
    after, before = lax.rem(me + 1, count), lax.rem(me + count - 1, count)
    barrier = pltpu.get_barrier_semaphore()

    group = min(8, count)
    base = me - lax.rem(me, group)
    mates = [base + lax.rem(me - base + away, group) for away in range(1, group)]
    twins = [lax.rem(me + away, count) for away in range(group, count, group)]
    friends = [(other, orb) for other in mates + twins + [before, after]]
    friends += [(me, lax.rem(orb + away, orbs)) for away in range(1, orbs)]
    for friend in friends:
        pl.semaphore_signal(barrier, inc=1, device_id=friend, device_id_type=MESH)

    def rows_of(c, size):
        return pl.ds(pl.multiple_of(c * size, size), size)

    def load_orbitals(c):
        rows = rows_of(c, 256)
        return pltpu.make_async_copy(orb_hbm.at[:, rows], orb_ref.at[:, rows], load_sem.at[c])

    load_table = pltpu.make_async_copy(table_hbm, table_ref, load_sem.at[4])
    load_coupling = pltpu.make_async_copy(coupling_hbm, coupling_ref, load_sem.at[5])
    for c in range(4):
        load_orbitals(c).start()
    load_table.start()
    load_coupling.start()

    spread_basis(basis_ref, basis2_ref)
    for given, kept in ((pair_in, pair_ref), (coarse_in, coarse_ref), (transfer_in, transfer_ref)):
        for i in range(given.shape[0]):
            kept[i] = spread(given[i])
    mid_ref[224:256, :] = jnp.zeros((32, 128), BF)
    top_ref[48:128, :] = jnp.zeros((80, 128), BF)

    def moments_chunk(c, _):
        load_orbitals(c).wait()
        rows = rows_of(c, 256)
        inner = pl.ds(pl.multiple_of(64 + c * 256, 64), 256)
        for o in range(2):
            values = orb_ref[o, rows, :]
            dens_ref[inner, o * 256 : (o + 1) * 256] = (values * values).astype(BF)
        leaf = dot(dens_ref[inner, :], basis2_ref[...], NT).astype(BF)
        leaf_ref[pl.ds(pl.multiple_of(192 + c * 256, 64), 256), :] = leaf
        picked = dot(octant_picker(32, 4, 256), leaf).astype(BF)
        mid_ref[pl.ds(pl.multiple_of(48 + c * 32, 16), 32), :] = merge_up(picked, 32, transfer_ref)
        return 0

    lax.fori_loop(0, 4, moments_chunk, 0)

    def halo(number, ref, head, tail, rows, ahead):
        source, target, device = (tail, 0, after) if ahead else (head, tail + rows, before)
        return pltpu.make_async_remote_copy(
            src_ref=ref.at[pl.ds(source, rows)],
            dst_ref=ref.at[pl.ds(target, rows)],
            send_sem=halo_send.at[number],
            recv_sem=halo_recv.at[number],
            device_id=(device, orb),
            device_id_type=MESH,
        )

    halos = []
    for ref, head, tail, rows in (
        (dens_ref, 64, 1024, 64),
        (leaf_ref, 192, 1024, 192),
        (mid_ref, 48, 128, 48),
        (top_ref, 16, 16, 16),
    ):
        for ahead in (False, True):
            halos.append(halo(len(halos), ref, head, tail, rows, ahead))
    top = merge_up(dot(octant_picker(16, 2, 128), mid_ref[48:176, :]).astype(BF), 16, transfer_ref)
    top_ref[16:32, :] = top
    cube_ref[rows_of(me, 16), :] = merge_up(
        dot(octant_picker(16, 1, 16), top).astype(BF), 16, transfer_ref
    )

    def cube_copies(first, blocks, others, stage):
        block = cube_ref.at[pl.ds(pl.multiple_of(first * 16, 16), blocks * 16)]
        return [
            pltpu.make_async_remote_copy(
                src_ref=block,
                dst_ref=block,
                send_sem=cube_send.at[stage + i],
                recv_sem=cube_recv.at[stage + i],
                device_id=(other, orb),
                device_id_type=MESH,
            )
            for i, other in enumerate(others)
        ]

    to_mates = cube_copies(me, 1, mates, 0)
    to_twins = cube_copies(base, group, twins, group - 1)

    def to_orbs(part, landing, send, recv, c, size):
        rows = rows_of(c, size)
        return [
            pltpu.make_async_remote_copy(
                src_ref=part.at[rows],
                dst_ref=landing.at[away - 1, rows],
                send_sem=send.at[away - 1, c],
                recv_sem=recv.at[away - 1, c],
                device_id=(me, lax.rem(orb + away, orbs)),
                device_id_type=MESH,
            )
            for away in range(1, orbs)
        ]

    load_table.wait()
    load_coupling.wait()

    def near_chunk(i, _):
        c = lax.rem(i + 1, 4)

        @pl.when(i == 1)
        def _():
            pl.semaphore_wait(barrier, len(friends))
            for copy in halos + to_mates:
                copy.start()

        @pl.when(i >= 1)
        def _():
            for copy in to_orbs(near_part, near_other, near_send, near_recv, i, 256):
                copy.start()

        @pl.when(i == 2)
        def _():
            for copy in halos[0:2] + to_mates:
                copy.wait()
            for copy in to_twins:
                copy.start()

        for r in range(16):
            turned_ref[i * 16 + r] = coupling_ref[i * 16 + r].astype(F32).T

        for part in range(2):
            base = pl.multiple_of(c * 256 + part * 128, 128)
            place = as_place((near_list[:, pl.ds(base, 128)].T + (64 + 128 * part)) & 255)
            for first in range(0, 27, 3):
                hot = one_hot(place, first, 3, 128, 256)
                for o in range(2):
                    source = dens_ref[pl.ds(base, 256), o * 256 : (o + 1) * 256]
                    at = o * 256 + part * 128
                    picked = dot(hot, source).astype(BF)
                    for k in range(3):
                        near_pick[at : at + 128, (first + k) * 256 : (first + k + 1) * 256] = picked[
                            k * 128 : (k + 1) * 128
                        ]
        total = None
        for k in range(27):
            part = dot(near_pick[:, k * 256 : (k + 1) * 256], table_ref[k], NT)
            total = part if total is None else total + part
        rows = rows_of(c, 256)
        near_ref[rows, 0:256] = total[:256]
        near_ref[rows, 256:512] = total[256:]
        near_part[rows, :] = (total[:256] + total[256:]).astype(BF)
        return 0

    lax.fori_loop(0, 4, near_chunk, 0)
    for copy in to_orbs(near_part, near_other, near_send, near_recv, 0, 256):
        copy.start()

    for k in range(108):
        weight_ref[:, k * 128 : (k + 1) * 128] = spread(turned_ref[:, k, :].astype(BF))
    for copy in halos[2:8]:
        copy.wait()

    def pick(place, rows, at, table):
        number = 128 // rows
        place = as_place(place)
        for first in range(0, 108, number):
            number = min(number, 108 - first)
            hot = one_hot(place, first, number, rows, table.shape[0])
            picked = dot(hot, table).astype(BF)
            for k in range(number):
                far_pick[at : at + rows, (first + k) * 128 : (first + k + 1) * 128] = picked[
                    k * rows : (k + 1) * rows
                ]

    mid_place = mid_list[...].T - (me * 128 - 48)
    pick(mid_place[0:64], 64, 0, mid_ref[...])
    pick(mid_place[64:128], 64, 64, mid_ref[...])
    pick(top_list[...] - (me * 16 - 16), 16, 128, top_ref[...])
    far = dot(far_pick[0:144, :], weight_ref[...], NT)

    for copy in to_twins:
        copy.wait()
    row, col = iota((64, cube_ref.shape[0]), 0), iota((64, cube_ref.shape[0]), 1)
    cubes = dot(ones_where(col == 16 * (row // 2) + row % 2), cube_ref[...]).astype(BF)
    row, col = iota((64, 64), 0), iota((64, 64), 1)
    child = [ones_where(col == 2 * row + p) for p in range(2)]
    mother = [ones_where((col == row // 2) & (row % 2 == p)) for p in range(2)]
    shift = [
        ones_where((col == row - 3) & (row % 2 == 1)),
        ones_where(col == row - 2),
        ones_where(col == row + 2),
        ones_where((col == row + 3) & (row % 2 == 0)),
    ]
    levels = [cubes]
    for _ in range(6):
        total = None
        for p in range(2):
            part = dot(dot(child[p], levels[-1]).astype(BF), pair_ref[p])
            total = part if total is None else total + part
        levels.append(total.astype(BF))
    coeffs = None
    for depth in range(6, -1, -1):
        total = None
        for w in range(4):
            part = dot(dot(shift[w], levels[depth]).astype(BF), coarse_ref[w], NT)
            total = part if total is None else total + part
        total = total * (0.5 ** (3 + depth))
        if coeffs is not None:
            for p in range(2):
                total = total + dot(dot(mother[p], coeffs).astype(BF), pair_ref[p], NT)
        coeffs = total.astype(BF)

    def split_down(coeffs, half, first, start, rows):
        parents = coeffs.shape[0]
        side = 2 * half
        row, col = iota((rows, parents), 0) + start, iota((rows, parents), 1)
        z, y, x = row // (side * side), (row // side) % side, row % side
        parent = ((z // 2) * half + y // 2) * half + x // 2 + first
        pulled = dot(ones_where(col == parent), coeffs).astype(BF)
        r = iota((rows, 128), 0) + start
        octant = 4 * ((r // (side * side)) % 2) + 2 * ((r // side) % 2) + r % 2
        total = None
        for o in range(8):
            part = dot(jnp.where(octant == o, pulled, jnp.zeros_like(pulled)), transfer_ref[o], NT)
            total = part if total is None else total + part
        return total

    top = 0.25 * far[128:144] + split_down(coeffs, 1, 2 * me, 0, 16)
    mid = 0.5 * far[0:128] + split_down(top.astype(BF), 2, 0, 0, 128)
    mid_ref[0:128, :] = mid.astype(BF)

    def leaf_chunk(c, _):
        for half in range(2):
            start = pl.multiple_of(c * 256 + half * 128, 128)
            offset = (leaf_list[:, pl.ds(start, 128)].T - c * 256 - half * 128 + 192) & 1023
            for layer in range(2):
                base = pl.multiple_of(start + layer * 64, 64)
                place = (offset[layer * 64 : (layer + 1) * 64] - 64 * layer) & 1023
                place = jnp.where(place < 128, place, place - 192)
                table = jnp.concatenate(
                    [leaf_ref[pl.ds(base, 128), :], leaf_ref[pl.ds(base + 320, 128), :]], axis=0
                )
                pick(place, 64, half * 128 + layer * 64, table)
        leaf = dot(far_pick[...], weight_ref[...], NT) + split_down(mid_ref[0:128, :], 4, 0, c * 256, 256)
        leaf = leaf.astype(BF)
        coeff_ref[rows_of(c, 256), :] = leaf
        wide = leaf.astype(F32)
        wide = wide + pltpu.roll(wide, 64, 1)
        packed = jnp.where(iota((128, 128), 1) < 64, wide[0:128], wide[128:256])
        coeff_part[rows_of(c, 128), :] = packed.astype(BF)
        for copy in to_orbs(coeff_part, coeff_other, coeff_send, coeff_recv, c, 128):
            copy.start()
        return 0

    lax.fori_loop(0, 4, leaf_chunk, 0)

    def change_chunk(c, _):
        for copy in to_orbs(near_part, near_other, near_send, near_recv, c, 256):
            copy.wait()
        for copy in to_orbs(coeff_part, coeff_other, coeff_send, coeff_recv, c, 128):
            copy.wait()
        rows, packed_rows = rows_of(c, 256), rows_of(c, 128)
        packed = coeff_part[packed_rows, :].astype(F32)
        hartree = near_part[rows, :].astype(F32)
        for away in range(orbs - 1):
            packed = packed + coeff_other[away, packed_rows, :].astype(F32)
            hartree = hartree + near_other[away, rows, :].astype(F32)
        both = dot(packed.astype(BF), basis2_ref[...])
        hartree = hartree + jnp.concatenate([both[:, :256], both[:, 256:]], axis=0)
        potential = near_ref[rows, :] + dot(coeff_ref[rows, :], basis2_ref[...])
        for o in range(2):
            out_ref[o, rows, :] = hartree - potential[:, o * 256 : (o + 1) * 256]
        return 0

    lax.fori_loop(0, 4, change_chunk, 0)


def shards(
    orbitals, near_source, far_leaf, far_mid, far_top, leaf_basis, near_table, transfer, coupling, pair_transfer,
    coarse_coupling,
):
    count, orbs = lax.axis_size("space"), lax.axis_size("orb")
    near_by, here = pl.BlockSpec(memory_space=pl.ANY), pl.BlockSpec(memory_space=pltpu.VMEM)
    change = pl.pallas_call(
        step_kernel,
        in_specs=[near_by, here, here, here, here, here, near_by, here, near_by, here, here],
        out_specs=here,
        out_shape=jax.ShapeDtypeStruct((2, 1024, 256), F32),
        scratch_shapes=[
            pltpu.VMEM((2, 1024, 256), F32),
            pltpu.VMEM((27, 256, 256), BF),
            pltpu.VMEM((64, 64, 108), BF),
            pltpu.VMEM((64, 108, 64), F32),
            pltpu.VMEM((1152, 512), BF),
            pltpu.VMEM((1408, 128), BF),
            pltpu.VMEM((256, 128), BF),
            pltpu.VMEM((128, 128), BF),
            pltpu.VMEM((count * 16, 128), BF),
            pltpu.VMEM((128, 512), BF),
            pltpu.VMEM((8, 128, 128), BF),
            pltpu.VMEM((2, 128, 128), BF),
            pltpu.VMEM((4, 128, 128), BF),
            pltpu.VMEM((128, 108 * 128), BF),
            pltpu.VMEM((512, 27 * 256), BF),
            pltpu.VMEM((256, 108 * 128), BF),
            pltpu.VMEM((1024, 512), F32),
            pltpu.VMEM((1024, 256), BF),
            pltpu.VMEM((orbs - 1, 1024, 256), BF),
            pltpu.VMEM((1024, 128), BF),
            pltpu.VMEM((512, 128), BF),
            pltpu.VMEM((orbs - 1, 512, 128), BF),
            pltpu.SemaphoreType.DMA((6,)),
            pltpu.SemaphoreType.DMA((8,)),
            pltpu.SemaphoreType.DMA((8,)),
            pltpu.SemaphoreType.DMA((16,)),
            pltpu.SemaphoreType.DMA((16,)),
            pltpu.SemaphoreType.DMA((orbs - 1, 4)),
            pltpu.SemaphoreType.DMA((orbs - 1, 4)),
            pltpu.SemaphoreType.DMA((orbs - 1, 4)),
            pltpu.SemaphoreType.DMA((orbs - 1, 4)),
        ],
        compiler_params=pltpu.CompilerParams(vmem_limit_bytes=48 << 20, collective_id=0, has_side_effects=True),
        cost_estimate=pl.CostEstimate(flops=36_000_000_000, bytes_accessed=12 << 20, transcendentals=0),
        name="step",
    )(
        orbitals, near_source.T, far_leaf.T, far_mid.T, far_top, leaf_basis, near_table, transfer,
        jnp.transpose(coupling, (1, 2, 0)), pair_transfer, coarse_coupling,
    )
    return orbitals - RELAX_STEP * change * orbitals


def solution(mesh):
    placed = (P("orb", "space", None),) + (P("space", None),) * 4 + (P(),) * 6
    return jax.shard_map(
        shards, mesh=mesh, in_specs=placed, out_specs=P("orb", "space", None), check_vma=False
    )
```

```python
import jax
import jax.numpy as jnp
from jax import lax
from jax.experimental import pallas as pl
from jax.experimental.pallas import tpu as pltpu
from jax.sharding import PartitionSpec as P

BF = jnp.bfloat16
F32 = jnp.float32
NN = (((1,), (0,)), ((), ()))
NT = (((1,), (1,)), ((), ()))
RELAX_STEP = 0.1
MESH = pl.DeviceIdType.MESH


def dot(a, b, dims=NN):
    return lax.dot_general(a, b, dims, preferred_element_type=F32)


def iota(shape, dim):
    return lax.broadcasted_iota(jnp.int32, shape, dim)


def ones_where(mask):
    return jnp.where(mask, 1.0, 0.0).astype(BF)


def one_hot(places, first, number, rows, width):
    lane = iota((rows, width), 1).astype(BF)
    found = [
        jnp.where(lane == places[:, k : k + 1], BF(1), BF(0)) for k in range(first, first + number)
    ]
    return jnp.concatenate(found, axis=0)


def as_place(numbers):
    return numbers.astype(F32).astype(BF)


def octant_picker(parents, half, width):
    row, col = iota((8 * parents, width), 0), iota((8 * parents, width), 1)
    octant, b = row // parents, row % parents
    z, y, x = b // (half * half), (b // half) % half, b % half
    dz, dy, dx = octant // 4, (octant // 2) % 2, octant % 2
    side = 2 * half
    child = ((2 * z + dz) * side + 2 * y + dy) * side + 2 * x + dx
    return ones_where(child == col)


def merge_up(picked, parents, transfer_ref):
    total = None
    for octant in range(8):
        part = dot(picked[octant * parents : (octant + 1) * parents], transfer_ref[octant])
        total = part if total is None else total + part
    return total.astype(BF)


def spread(matrix):
    zero = jnp.zeros_like(matrix)
    top = jnp.concatenate([matrix, zero], axis=1)
    return jnp.concatenate([top, jnp.concatenate([zero, matrix], axis=1)], axis=0)


def spread_basis(basis_ref, basis2_ref):
    basis2_ref[...] = jnp.zeros((128, 512), BF)
    basis2_ref[0:64, 0:256] = basis_ref[...]
    basis2_ref[64:128, 256:512] = basis_ref[...]


def step_kernel(
    orb_hbm, near_list, leaf_list, mid_list, top_list, basis_ref, table_hbm, transfer_in, coupling_hbm, pair_in, coarse_in,
    out_ref,
    orb_ref, table_ref, coupling_ref, dens_ref, leaf_ref, mid_ref, top_ref, cube_ref, basis2_ref, transfer_ref, pair_ref,
    coarse_ref, weight_ref, near_pick, far_pick, near_ref, near_part, near_other, far_ref, coeff_ref, coeff_part, coeff_other,
    load_sem, halo_send, halo_recv, cube_send, cube_recv, near_send, near_recv, coeff_send, coeff_recv,
):
    me, orb = lax.axis_index("space"), lax.axis_index("orb")
    count, orbs = lax.axis_size("space"), lax.axis_size("orb")
    after, before = lax.rem(me + 1, count), lax.rem(me + count - 1, count)
    barrier = pltpu.get_barrier_semaphore()

    group = min(8, count)
    base = me - lax.rem(me, group)
    mates = [base + lax.rem(me - base + away, group) for away in range(1, group)]
    twins = [lax.rem(me + away, count) for away in range(group, count, group)]
    friends = [(other, orb) for other in mates + twins + [before, after]]
    friends += [(me, lax.rem(orb + away, orbs)) for away in range(1, orbs)]
    for friend in friends:
        pl.semaphore_signal(barrier, inc=1, device_id=friend, device_id_type=MESH)

    def rows_of(c, size):
        return pl.ds(pl.multiple_of(c * size, size), size)

    def load_orbitals(c):
        rows = rows_of(c, 256)
        return pltpu.make_async_copy(orb_hbm.at[:, rows], orb_ref.at[:, rows], load_sem.at[c])

    load_table = pltpu.make_async_copy(table_hbm, table_ref, load_sem.at[4])
    load_coupling = pltpu.make_async_copy(coupling_hbm, coupling_ref, load_sem.at[5])
    for c in range(4):
        load_orbitals(c).start()
    load_table.start()
    load_coupling.start()

    spread_basis(basis_ref, basis2_ref)
    for given, kept in ((pair_in, pair_ref), (coarse_in, coarse_ref), (transfer_in, transfer_ref)):
        for i in range(given.shape[0]):
            kept[i] = spread(given[i])
    mid_ref[224:256, :] = jnp.zeros((32, 128), BF)
    top_ref[48:128, :] = jnp.zeros((80, 128), BF)

    def moments_chunk(c, _):
        load_orbitals(c).wait()
        rows = rows_of(c, 256)
        inner = pl.ds(pl.multiple_of(64 + c * 256, 64), 256)
        for o in range(2):
            values = orb_ref[o, rows, :]
            dens_ref[inner, o * 256 : (o + 1) * 256] = (values * values).astype(BF)
        leaf = dot(dens_ref[inner, :], basis2_ref[...], NT).astype(BF)
        leaf_ref[pl.ds(pl.multiple_of(192 + c * 256, 64), 256), :] = leaf
        picked = dot(octant_picker(32, 4, 256), leaf).astype(BF)
        mid_ref[pl.ds(pl.multiple_of(48 + c * 32, 16), 32), :] = merge_up(picked, 32, transfer_ref)
        return 0

    lax.fori_loop(0, 4, moments_chunk, 0)

    def halo(number, ref, head, tail, rows, ahead):
        source, target, device = (tail, 0, after) if ahead else (head, tail + rows, before)
        return pltpu.make_async_remote_copy(
            src_ref=ref.at[pl.ds(source, rows)],
            dst_ref=ref.at[pl.ds(target, rows)],
            send_sem=halo_send.at[number],
            recv_sem=halo_recv.at[number],
            device_id=(device, orb),
            device_id_type=MESH,
        )

    halos = []
    for ref, head, tail, rows in (
        (dens_ref, 64, 1024, 64),
        (leaf_ref, 192, 1024, 192),
        (mid_ref, 48, 128, 48),
        (top_ref, 16, 16, 16),
    ):
        for ahead in (False, True):
            halos.append(halo(len(halos), ref, head, tail, rows, ahead))
    top = merge_up(dot(octant_picker(16, 2, 128), mid_ref[48:176, :]).astype(BF), 16, transfer_ref)
    top_ref[16:32, :] = top
    cube_ref[rows_of(me, 16), :] = merge_up(
        dot(octant_picker(16, 1, 16), top).astype(BF), 16, transfer_ref
    )

    def cube_copies(first, blocks, others, stage):
        block = cube_ref.at[pl.ds(pl.multiple_of(first * 16, 16), blocks * 16)]
        return [
            pltpu.make_async_remote_copy(
                src_ref=block,
                dst_ref=block,
                send_sem=cube_send.at[stage + i],
                recv_sem=cube_recv.at[stage + i],
                device_id=(other, orb),
                device_id_type=MESH,
            )
            for i, other in enumerate(others)
        ]

    to_mates = cube_copies(me, 1, mates, 0)
    to_twins = cube_copies(base, group, twins, group - 1)

    def to_orbs(part, landing, send, recv, c, size):
        rows = rows_of(c, size)
        return [
            pltpu.make_async_remote_copy(
                src_ref=part.at[rows],
                dst_ref=landing.at[away - 1, rows],
                send_sem=send.at[away - 1, c],
                recv_sem=recv.at[away - 1, c],
                device_id=(me, lax.rem(orb + away, orbs)),
                device_id_type=MESH,
            )
            for away in range(1, orbs)
        ]

    load_table.wait()
    load_coupling.wait()

    def near_chunk(i, _):
        c = lax.rem(i + 1, 4)

        @pl.when(i == 1)
        def _():
            pl.semaphore_wait(barrier, len(friends))
            for copy in halos + to_mates:
                copy.start()

        @pl.when(i >= 1)
        def _():
            for copy in to_orbs(near_part, near_other, near_send, near_recv, i, 256):
                copy.start()

        @pl.when(i == 2)
        def _():
            for copy in halos[0:2] + to_mates:
                copy.wait()
            for copy in to_twins:
                copy.start()

        for part in range(2):
            base = pl.multiple_of(c * 256 + part * 128, 128)
            place = as_place((near_list[:, pl.ds(base, 128)].T + (64 + 128 * part)) & 255)
            for first in range(0, 27, 3):
                hot = one_hot(place, first, 3, 128, 256)
                for o in range(2):
                    source = dens_ref[pl.ds(base, 256), o * 256 : (o + 1) * 256]
                    at = o * 256 + part * 128
                    picked = dot(hot, source).astype(BF)
                    for k in range(3):
                        near_pick[at : at + 128, (first + k) * 256 : (first + k + 1) * 256] = picked[
                            k * 128 : (k + 1) * 128
                        ]
        total = None
        for k in range(27):
            part = dot(near_pick[:, k * 256 : (k + 1) * 256], table_ref[k], NT)
            total = part if total is None else total + part
        rows = rows_of(c, 256)
        near_ref[rows, 0:256] = total[:256]
        near_ref[rows, 256:512] = total[256:]
        near_part[rows, :] = (total[:256] + total[256:]).astype(BF)
        return 0

    lax.fori_loop(0, 2, near_chunk, 0)
    for k in range(108):
        weight_ref[:, k * 128 : (k + 1) * 128] = spread(coupling_ref[k])

    def pick(place, rows, at, table):
        number = 128 // rows
        place = as_place(place)
        for first in range(0, 108, number):
            number = min(number, 108 - first)
            hot = one_hot(place, first, number, rows, table.shape[0])
            picked = dot(hot, table).astype(BF)
            for k in range(number):
                far_pick[at : at + rows, (first + k) * 128 : (first + k + 1) * 128] = picked[
                    k * rows : (k + 1) * rows
                ]

    def far_chunk(c):
        for half in range(2):
            start = pl.multiple_of(c * 256 + half * 128, 128)
            offset = (leaf_list[:, pl.ds(start, 128)].T - start + 192) & 1023
            for layer in range(2):
                base = pl.multiple_of(start + layer * 64, 64)
                table = jnp.concatenate(
                    [leaf_ref[pl.ds(base, 128), :], leaf_ref[pl.ds(base + 320, 128), :]], axis=0
                )
                place = (offset[layer * 64 : (layer + 1) * 64] - 64 * layer) & 1023
                place = jnp.where(place < 128, place, place - 192)
                pick(place, 64, half * 128 + layer * 64, table)
        far_ref[rows_of(c, 256), :] = dot(far_pick[...], weight_ref[...], NT)

    def inner_far(i, _):
        far_chunk(i + 1)
        return 0

    lax.fori_loop(0, 2, inner_far, 0)
    lax.fori_loop(2, 4, near_chunk, 0)
    for copy in to_orbs(near_part, near_other, near_send, near_recv, 0, 256):
        copy.start()

    for copy in halos[2:8]:
        copy.wait()

    mid_place = mid_list[...].T - (me * 128 - 48)
    pick(mid_place[0:64], 64, 0, mid_ref[...])
    pick(mid_place[64:128], 64, 64, mid_ref[...])
    pick(top_list[...] - (me * 16 - 16), 16, 128, top_ref[...])
    far = dot(far_pick[0:144, :], weight_ref[...], NT)

    for copy in to_twins:
        copy.wait()
    row, col = iota((64, cube_ref.shape[0]), 0), iota((64, cube_ref.shape[0]), 1)
    cubes = dot(ones_where(col == 16 * (row // 2) + row % 2), cube_ref[...]).astype(BF)
    row, col = iota((64, 64), 0), iota((64, 64), 1)
    child = [ones_where(col == 2 * row + p) for p in range(2)]
    mother = [ones_where((col == row // 2) & (row % 2 == p)) for p in range(2)]
    shift = [
        ones_where((col == row - 3) & (row % 2 == 1)),
        ones_where(col == row - 2),
        ones_where(col == row + 2),
        ones_where((col == row + 3) & (row % 2 == 0)),
    ]
    levels = [cubes]
    for _ in range(6):
        total = None
        for p in range(2):
            part = dot(dot(child[p], levels[-1]).astype(BF), pair_ref[p])
            total = part if total is None else total + part
        levels.append(total.astype(BF))
    coeffs = None
    for depth in range(6, -1, -1):
        total = None
        for w in range(4):
            part = dot(dot(shift[w], levels[depth]).astype(BF), coarse_ref[w], NT)
            total = part if total is None else total + part
        total = total * (0.5 ** (3 + depth))
        if coeffs is not None:
            for p in range(2):
                total = total + dot(dot(mother[p], coeffs).astype(BF), pair_ref[p], NT)
        coeffs = total.astype(BF)

    def split_down(coeffs, half, first, start, rows):
        parents = coeffs.shape[0]
        side = 2 * half
        row, col = iota((rows, parents), 0) + start, iota((rows, parents), 1)
        z, y, x = row // (side * side), (row // side) % side, row % side
        parent = ((z // 2) * half + y // 2) * half + x // 2 + first
        pulled = dot(ones_where(col == parent), coeffs).astype(BF)
        r = iota((rows, 128), 0) + start
        octant = 4 * ((r // (side * side)) % 2) + 2 * ((r // side) % 2) + r % 2
        total = None
        for o in range(8):
            part = dot(jnp.where(octant == o, pulled, jnp.zeros_like(pulled)), transfer_ref[o], NT)
            total = part if total is None else total + part
        return total

    top = 0.25 * far[128:144] + split_down(coeffs, 1, 2 * me, 0, 16)
    mid = 0.5 * far[0:128] + split_down(top.astype(BF), 2, 0, 0, 128)
    mid_ref[0:128, :] = mid.astype(BF)

    def finish_chunk(c):
        leaf = far_ref[rows_of(c, 256), :] + split_down(mid_ref[0:128, :], 4, 0, c * 256, 256)
        leaf = leaf.astype(BF)
        coeff_ref[rows_of(c, 256), :] = leaf
        wide = leaf.astype(F32)
        wide = wide + pltpu.roll(wide, 64, 1)
        packed = jnp.where(iota((128, 128), 1) < 64, wide[0:128], wide[128:256])
        coeff_part[rows_of(c, 128), :] = packed.astype(BF)
        for copy in to_orbs(coeff_part, coeff_other, coeff_send, coeff_recv, c, 128):
            copy.start()

    def finish_inner(i, _):
        finish_chunk(i + 1)
        return 0

    def finish_outer(i, _):
        c = lax.rem(i + 1, 4)
        far_chunk(c)
        finish_chunk(c)
        return 0

    lax.fori_loop(0, 2, finish_inner, 0)
    lax.fori_loop(2, 4, finish_outer, 0)

    def change_chunk(c, _):
        for copy in to_orbs(near_part, near_other, near_send, near_recv, c, 256):
            copy.wait()
        for copy in to_orbs(coeff_part, coeff_other, coeff_send, coeff_recv, c, 128):
            copy.wait()
        rows, packed_rows = rows_of(c, 256), rows_of(c, 128)
        packed = coeff_part[packed_rows, :].astype(F32)
        hartree = near_part[rows, :].astype(F32)
        for away in range(orbs - 1):
            packed = packed + coeff_other[away, packed_rows, :].astype(F32)
            hartree = hartree + near_other[away, rows, :].astype(F32)
        both = dot(packed.astype(BF), basis2_ref[...])
        hartree = hartree + jnp.concatenate([both[:, :256], both[:, 256:]], axis=0)
        potential = near_ref[rows, :] + dot(coeff_ref[rows, :], basis2_ref[...])
        for o in range(2):
            out_ref[o, rows, :] = hartree - potential[:, o * 256 : (o + 1) * 256]
        return 0

    lax.fori_loop(0, 4, change_chunk, 0)


def shards(
    orbitals, near_source, far_leaf, far_mid, far_top, leaf_basis, near_table, transfer, coupling, pair_transfer,
    coarse_coupling,
):
    count, orbs = lax.axis_size("space"), lax.axis_size("orb")
    near_by, here = pl.BlockSpec(memory_space=pl.ANY), pl.BlockSpec(memory_space=pltpu.VMEM)
    change = pl.pallas_call(
        step_kernel,
        in_specs=[near_by, here, here, here, here, here, near_by, here, near_by, here, here],
        out_specs=here,
        out_shape=jax.ShapeDtypeStruct((2, 1024, 256), F32),
        scratch_shapes=[
            pltpu.VMEM((2, 1024, 256), F32),
            pltpu.VMEM((27, 256, 256), BF),
            pltpu.VMEM((108, 64, 64), BF),
            pltpu.VMEM((1152, 512), BF),
            pltpu.VMEM((1408, 128), BF),
            pltpu.VMEM((256, 128), BF),
            pltpu.VMEM((128, 128), BF),
            pltpu.VMEM((count * 16, 128), BF),
            pltpu.VMEM((128, 512), BF),
            pltpu.VMEM((8, 128, 128), BF),
            pltpu.VMEM((2, 128, 128), BF),
            pltpu.VMEM((4, 128, 128), BF),
            pltpu.VMEM((128, 108 * 128), BF),
            pltpu.VMEM((512, 27 * 256), BF),
            pltpu.VMEM((256, 108 * 128), BF),
            pltpu.VMEM((1024, 512), F32),
            pltpu.VMEM((1024, 256), BF),
            pltpu.VMEM((orbs - 1, 1024, 256), BF),
            pltpu.VMEM((1024, 128), F32),
            pltpu.VMEM((1024, 128), BF),
            pltpu.VMEM((512, 128), BF),
            pltpu.VMEM((orbs - 1, 512, 128), BF),
            pltpu.SemaphoreType.DMA((6,)),
            pltpu.SemaphoreType.DMA((8,)),
            pltpu.SemaphoreType.DMA((8,)),
            pltpu.SemaphoreType.DMA((16,)),
            pltpu.SemaphoreType.DMA((16,)),
            pltpu.SemaphoreType.DMA((orbs - 1, 4)),
            pltpu.SemaphoreType.DMA((orbs - 1, 4)),
            pltpu.SemaphoreType.DMA((orbs - 1, 4)),
            pltpu.SemaphoreType.DMA((orbs - 1, 4)),
        ],
        compiler_params=pltpu.CompilerParams(vmem_limit_bytes=48 << 20, collective_id=0, has_side_effects=True),
        cost_estimate=pl.CostEstimate(flops=36_000_000_000, bytes_accessed=12 << 20, transcendentals=0),
        name="step",
    )(
        orbitals, near_source.T, far_leaf.T, far_mid.T, far_top, leaf_basis, near_table, transfer,
        coupling, pair_transfer, coarse_coupling,
    )
    return orbitals - RELAX_STEP * change * orbitals


def solution(mesh):
    placed = (P("orb", "space", None),) + (P("space", None),) * 4 + (P(),) * 6
    return jax.shard_map(
        shards, mesh=mesh, in_specs=placed, out_specs=P("orb", "space", None), check_vma=False
    )
```

```python
import jax
import jax.numpy as jnp
from jax import lax
from jax.experimental import pallas as pl
from jax.experimental.pallas import tpu as pltpu
from jax.sharding import PartitionSpec as P

BF = jnp.bfloat16
F32 = jnp.float32
NN = (((1,), (0,)), ((), ()))
NT = (((1,), (1,)), ((), ()))
RELAX_STEP = 0.1
MESH = pl.DeviceIdType.MESH


def dot(a, b, dims=NN):
    return lax.dot_general(a, b, dims, preferred_element_type=F32)


def iota(shape, dim):
    return lax.broadcasted_iota(jnp.int32, shape, dim)


def ones_where(mask):
    return jnp.where(mask, 1.0, 0.0).astype(BF)


def one_hot(places, first, number, rows, width):
    lane = iota((rows, width), 1).astype(BF)
    found = [
        jnp.where(lane == places[:, k : k + 1], BF(1), BF(0)) for k in range(first, first + number)
    ]
    return jnp.concatenate(found, axis=0)


def as_place(numbers):
    return numbers.astype(F32).astype(BF)


def octant_picker(parents, half, width):
    row, col = iota((8 * parents, width), 0), iota((8 * parents, width), 1)
    octant, b = row // parents, row % parents
    z, y, x = b // (half * half), (b // half) % half, b % half
    dz, dy, dx = octant // 4, (octant // 2) % 2, octant % 2
    side = 2 * half
    child = ((2 * z + dz) * side + 2 * y + dy) * side + 2 * x + dx
    return ones_where(child == col)


def merge_up(picked, parents, transfer_ref):
    total = None
    for octant in range(8):
        part = dot(picked[octant * parents : (octant + 1) * parents], transfer_ref[octant])
        total = part if total is None else total + part
    return total.astype(BF)


def spread(matrix):
    zero = jnp.zeros_like(matrix)
    top = jnp.concatenate([matrix, zero], axis=1)
    return jnp.concatenate([top, jnp.concatenate([zero, matrix], axis=1)], axis=0)


def spread_basis(basis_ref, basis2_ref):
    basis2_ref[...] = jnp.zeros((128, 512), BF)
    basis2_ref[0:64, 0:256] = basis_ref[...]
    basis2_ref[64:128, 256:512] = basis_ref[...]


def step_kernel(
    orb_hbm, near_list, leaf_list, mid_list, top_list, basis_ref, table_hbm, transfer_in, coupling_hbm, pair_in, coarse_in,
    out_ref,
    orb_ref, table_ref, coupling_ref, dens_ref, leaf_ref, mid_ref, top_ref, cube_ref, basis2_ref, transfer_ref, pair_ref,
    coarse_ref, weight_ref, near_pick, far_pick, near_ref, near_part, near_other, far_ref, coeff_ref, coeff_part, coeff_other,
    load_sem, halo_send, halo_recv, cube_send, cube_recv, near_send, near_recv, coeff_send, coeff_recv,
):
    me, orb = lax.axis_index("space"), lax.axis_index("orb")
    count, orbs = lax.axis_size("space"), lax.axis_size("orb")
    after, before = lax.rem(me + 1, count), lax.rem(me + count - 1, count)
    barrier = pltpu.get_barrier_semaphore()

    group = min(8, count)
    base = me - lax.rem(me, group)
    mates = [base + lax.rem(me - base + away, group) for away in range(1, group)]
    twins = [lax.rem(me + away, count) for away in range(group, count, group)]
    friends = [(other, orb) for other in mates + twins + [before, after]]
    friends += [(me, lax.rem(orb + away, orbs)) for away in range(1, orbs)]
    for friend in friends:
        pl.semaphore_signal(barrier, inc=1, device_id=friend, device_id_type=MESH)

    def rows_of(c, size):
        return pl.ds(pl.multiple_of(c * size, size), size)

    def load_orbitals(c):
        rows = rows_of(c, 256)
        return pltpu.make_async_copy(orb_hbm.at[:, rows], orb_ref.at[:, rows], load_sem.at[c])

    load_table = pltpu.make_async_copy(table_hbm, table_ref, load_sem.at[4])
    load_coupling = pltpu.make_async_copy(coupling_hbm, coupling_ref, load_sem.at[5])
    for c in range(4):
        load_orbitals(c).start()
    load_table.start()
    load_coupling.start()

    spread_basis(basis_ref, basis2_ref)
    for given, kept in ((pair_in, pair_ref), (coarse_in, coarse_ref), (transfer_in, transfer_ref)):
        for i in range(given.shape[0]):
            kept[i] = spread(given[i])
    mid_ref[224:256, :] = jnp.zeros((32, 128), BF)
    top_ref[48:128, :] = jnp.zeros((80, 128), BF)

    def moments_chunk(c, _):
        load_orbitals(c).wait()
        rows = rows_of(c, 256)
        inner = pl.ds(pl.multiple_of(64 + c * 256, 64), 256)
        for o in range(2):
            values = orb_ref[o, rows, :]
            dens_ref[inner, o * 256 : (o + 1) * 256] = (values * values).astype(BF)
        leaf = dot(dens_ref[inner, :], basis2_ref[...], NT).astype(BF)
        leaf_ref[pl.ds(pl.multiple_of(192 + c * 256, 64), 256), :] = leaf
        picked = dot(octant_picker(32, 4, 256), leaf).astype(BF)
        mid_ref[pl.ds(pl.multiple_of(48 + c * 32, 16), 32), :] = merge_up(picked, 32, transfer_ref)
        return 0

    lax.fori_loop(0, 4, moments_chunk, 0)

    def halo(number, ref, head, tail, rows, ahead):
        source, target, device = (tail, 0, after) if ahead else (head, tail + rows, before)
        return pltpu.make_async_remote_copy(
            src_ref=ref.at[pl.ds(source, rows)],
            dst_ref=ref.at[pl.ds(target, rows)],
            send_sem=halo_send.at[number],
            recv_sem=halo_recv.at[number],
            device_id=(device, orb),
            device_id_type=MESH,
        )

    halos = []
    for ref, head, tail, rows in (
        (dens_ref, 64, 1024, 64),
        (leaf_ref, 192, 1024, 192),
        (mid_ref, 48, 128, 48),
        (top_ref, 16, 16, 16),
    ):
        for ahead in (False, True):
            halos.append(halo(len(halos), ref, head, tail, rows, ahead))
    top = merge_up(dot(octant_picker(16, 2, 128), mid_ref[48:176, :]).astype(BF), 16, transfer_ref)
    top_ref[16:32, :] = top
    cube_ref[rows_of(me, 16), :] = merge_up(
        dot(octant_picker(16, 1, 16), top).astype(BF), 16, transfer_ref
    )

    def cube_copies(first, blocks, others, stage):
        block = cube_ref.at[pl.ds(pl.multiple_of(first * 16, 16), blocks * 16)]
        return [
            pltpu.make_async_remote_copy(
                src_ref=block,
                dst_ref=block,
                send_sem=cube_send.at[stage + i],
                recv_sem=cube_recv.at[stage + i],
                device_id=(other, orb),
                device_id_type=MESH,
            )
            for i, other in enumerate(others)
        ]

    to_mates = cube_copies(me, 1, mates, 0)
    to_twins = cube_copies(base, group, twins, group - 1)

    def to_orbs(part, landing, send, recv, c, size):
        rows = rows_of(c, size)
        return [
            pltpu.make_async_remote_copy(
                src_ref=part.at[rows],
                dst_ref=landing.at[away - 1, rows],
                send_sem=send.at[away - 1, c],
                recv_sem=recv.at[away - 1, c],
                device_id=(me, lax.rem(orb + away, orbs)),
                device_id_type=MESH,
            )
            for away in range(1, orbs)
        ]

    load_table.wait()
    load_coupling.wait()

    def near_chunk(i, _):
        c = lax.rem(i + 1, 4)

        @pl.when(i == 1)
        def _():
            pl.semaphore_wait(barrier, len(friends))
            for copy in halos + to_mates:
                copy.start()

        @pl.when(i >= 1)
        def _():
            for copy in to_orbs(near_part, near_other, near_send, near_recv, i, 256):
                copy.start()

        @pl.when(i == 2)
        def _():
            for copy in halos[0:2] + to_mates:
                copy.wait()
            for copy in to_twins:
                copy.start()

        for part in range(2):
            base = pl.multiple_of(c * 256 + part * 128, 128)
            place = as_place((near_list[:, pl.ds(base, 128)].T + (64 + 128 * part)) & 255)
            for first in range(0, 27, 3):
                hot = one_hot(place, first, 3, 128, 256)
                for o in range(2):
                    source = dens_ref[pl.ds(base, 256), o * 256 : (o + 1) * 256]
                    at = o * 256 + part * 128
                    picked = dot(hot, source).astype(BF)
                    for k in range(3):
                        near_pick[at : at + 128, (first + k) * 256 : (first + k + 1) * 256] = picked[
                            k * 128 : (k + 1) * 128
                        ]
        total = None
        for k in range(27):
            part = dot(near_pick[:, k * 256 : (k + 1) * 256], table_ref[k], NT)
            total = part if total is None else total + part
        rows = rows_of(c, 256)
        near_ref[rows, 0:256] = total[:256]
        near_ref[rows, 256:512] = total[256:]
        near_part[rows, :] = (total[:256] + total[256:]).astype(BF)
        return 0

    lax.fori_loop(0, 2, near_chunk, 0)
    for k in range(108):
        weight_ref[:, k * 128 : (k + 1) * 128] = spread(coupling_ref[k])

    def pick(place, rows, at, table, beside=iter(())):
        number = 128 // rows
        place = as_place(place)
        for first in range(0, 108, number):
            number = min(number, 108 - first)
            hot = one_hot(place, first, number, rows, table.shape[0])
            picked = dot(hot, table).astype(BF)
            for k in range(number):
                far_pick[at : at + rows, (first + k) * 128 : (first + k + 1) * 128] = picked[
                    k * rows : (k + 1) * rows
                ]
            next(beside, None)

    def far_chunk(c):
        for half in range(2):
            start = pl.multiple_of(c * 256 + half * 128, 128)
            offset = (leaf_list[:, pl.ds(start, 128)].T - start + 192) & 1023
            for layer in range(2):
                base = pl.multiple_of(start + layer * 64, 64)
                table = jnp.concatenate(
                    [leaf_ref[pl.ds(base, 128), :], leaf_ref[pl.ds(base + 320, 128), :]], axis=0
                )
                place = (offset[layer * 64 : (layer + 1) * 64] - 64 * layer) & 1023
                place = jnp.where(place < 128, place, place - 192)
                pick(place, 64, half * 128 + layer * 64, table)
        far_ref[rows_of(c, 256), :] = dot(far_pick[...], weight_ref[...], NT)

    def inner_far(i, _):
        far_chunk(i + 1)
        return 0

    lax.fori_loop(0, 2, inner_far, 0)
    lax.fori_loop(2, 4, near_chunk, 0)
    for copy in to_orbs(near_part, near_other, near_send, near_recv, 0, 256):
        copy.start()

    for copy in halos[2:8]:
        copy.wait()

    for copy in to_twins:
        copy.wait()

    coarse_coeffs = []

    def coarse_tree():
        row, col = iota((64, cube_ref.shape[0]), 0), iota((64, cube_ref.shape[0]), 1)
        cubes = dot(ones_where(col == 16 * (row // 2) + row % 2), cube_ref[...]).astype(BF)
        row, col = iota((64, 64), 0), iota((64, 64), 1)
        child = [ones_where(col == 2 * row + p) for p in range(2)]
        mother = [ones_where((col == row // 2) & (row % 2 == p)) for p in range(2)]
        shift = [
            ones_where((col == row - 3) & (row % 2 == 1)),
            ones_where(col == row - 2),
            ones_where(col == row + 2),
            ones_where((col == row + 3) & (row % 2 == 0)),
        ]
        yield

        def coupled(level, depth):
            total = None
            for w in range(4):
                part = dot(dot(shift[w], level).astype(BF), coarse_ref[w], NT)
                total = part if total is None else total + part
            return total * (0.5 ** (3 + depth))

        level, coupled_levels = cubes, []
        for depth in range(6):
            picked = [dot(child[p], level).astype(BF) for p in range(2)]
            yield
            coupled_levels.append(coupled(level, depth))
            yield
            level = (dot(picked[0], pair_ref[0]) + dot(picked[1], pair_ref[1])).astype(BF)
            yield
        coeffs = coupled(level, 6).astype(BF)
        yield
        for depth in range(5, -1, -1):
            picked = [dot(mother[p], coeffs).astype(BF) for p in range(2)]
            yield
            total = coupled_levels[depth]
            for p in range(2):
                total = total + dot(picked[p], pair_ref[p], NT)
            coeffs = total.astype(BF)
            yield
        coarse_coeffs.append(coeffs)

    steps = coarse_tree()
    mid_place = mid_list[...].T - (me * 128 - 48)
    pick(mid_place[0:64], 64, 0, mid_ref[...], steps)
    pick(mid_place[64:128], 64, 64, mid_ref[...], steps)
    for _ in steps:
        pass
    coeffs = coarse_coeffs[0]
    pick(top_list[...] - (me * 16 - 16), 16, 128, top_ref[...])
    far = dot(far_pick[0:144, :], weight_ref[...], NT)

    def split_down(coeffs, half, first, start, rows):
        parents = coeffs.shape[0]
        side = 2 * half
        row, col = iota((rows, parents), 0) + start, iota((rows, parents), 1)
        z, y, x = row // (side * side), (row // side) % side, row % side
        parent = ((z // 2) * half + y // 2) * half + x // 2 + first
        pulled = dot(ones_where(col == parent), coeffs).astype(BF)
        r = iota((rows, 128), 0) + start
        octant = 4 * ((r // (side * side)) % 2) + 2 * ((r // side) % 2) + r % 2
        total = None
        for o in range(8):
            part = dot(jnp.where(octant == o, pulled, jnp.zeros_like(pulled)), transfer_ref[o], NT)
            total = part if total is None else total + part
        return total

    top = 0.25 * far[128:144] + split_down(coeffs, 1, 2 * me, 0, 16)
    mid = 0.5 * far[0:128] + split_down(top.astype(BF), 2, 0, 0, 128)
    mid_ref[0:128, :] = mid.astype(BF)

    def finish_chunk(c):
        leaf = far_ref[rows_of(c, 256), :] + split_down(mid_ref[0:128, :], 4, 0, c * 256, 256)
        leaf = leaf.astype(BF)
        coeff_ref[rows_of(c, 256), :] = leaf
        wide = leaf.astype(F32)
        wide = wide + pltpu.roll(wide, 64, 1)
        packed = jnp.where(iota((128, 128), 1) < 64, wide[0:128], wide[128:256])
        coeff_part[rows_of(c, 128), :] = packed.astype(BF)
        for copy in to_orbs(coeff_part, coeff_other, coeff_send, coeff_recv, c, 128):
            copy.start()

    def finish_inner(i, _):
        finish_chunk(i + 1)
        return 0

    def finish_outer(i, _):
        c = lax.rem(i + 1, 4)
        far_chunk(c)
        finish_chunk(c)
        return 0

    lax.fori_loop(0, 2, finish_inner, 0)
    lax.fori_loop(2, 4, finish_outer, 0)

    def change_chunk(i, _):
        c = lax.rem(i + 1, 4)
        for copy in to_orbs(near_part, near_other, near_send, near_recv, c, 256):
            copy.wait()
        for copy in to_orbs(coeff_part, coeff_other, coeff_send, coeff_recv, c, 128):
            copy.wait()
        rows, packed_rows = rows_of(c, 256), rows_of(c, 128)
        packed = coeff_part[packed_rows, :].astype(F32)
        hartree = near_part[rows, :].astype(F32)
        for away in range(orbs - 1):
            packed = packed + coeff_other[away, packed_rows, :].astype(F32)
            hartree = hartree + near_other[away, rows, :].astype(F32)
        both = dot(packed.astype(BF), basis2_ref[...])
        hartree = hartree + jnp.concatenate([both[:, :256], both[:, 256:]], axis=0)
        potential = near_ref[rows, :] + dot(coeff_ref[rows, :], basis2_ref[...])
        for o in range(2):
            out_ref[o, rows, :] = hartree - potential[:, o * 256 : (o + 1) * 256]
        return 0

    lax.fori_loop(0, 4, change_chunk, 0)


def shards(
    orbitals, near_source, far_leaf, far_mid, far_top, leaf_basis, near_table, transfer, coupling, pair_transfer,
    coarse_coupling,
):
    count, orbs = lax.axis_size("space"), lax.axis_size("orb")
    near_by, here = pl.BlockSpec(memory_space=pl.ANY), pl.BlockSpec(memory_space=pltpu.VMEM)
    change = pl.pallas_call(
        step_kernel,
        in_specs=[near_by, here, here, here, here, here, near_by, here, near_by, here, here],
        out_specs=here,
        out_shape=jax.ShapeDtypeStruct((2, 1024, 256), F32),
        scratch_shapes=[
            pltpu.VMEM((2, 1024, 256), F32),
            pltpu.VMEM((27, 256, 256), BF),
            pltpu.VMEM((108, 64, 64), BF),
            pltpu.VMEM((1152, 512), BF),
            pltpu.VMEM((1408, 128), BF),
            pltpu.VMEM((256, 128), BF),
            pltpu.VMEM((128, 128), BF),
            pltpu.VMEM((count * 16, 128), BF),
            pltpu.VMEM((128, 512), BF),
            pltpu.VMEM((8, 128, 128), BF),
            pltpu.VMEM((2, 128, 128), BF),
            pltpu.VMEM((4, 128, 128), BF),
            pltpu.VMEM((128, 108 * 128), BF),
            pltpu.VMEM((512, 27 * 256), BF),
            pltpu.VMEM((256, 108 * 128), BF),
            pltpu.VMEM((1024, 512), F32),
            pltpu.VMEM((1024, 256), BF),
            pltpu.VMEM((orbs - 1, 1024, 256), BF),
            pltpu.VMEM((1024, 128), F32),
            pltpu.VMEM((1024, 128), BF),
            pltpu.VMEM((512, 128), BF),
            pltpu.VMEM((orbs - 1, 512, 128), BF),
            pltpu.SemaphoreType.DMA((6,)),
            pltpu.SemaphoreType.DMA((8,)),
            pltpu.SemaphoreType.DMA((8,)),
            pltpu.SemaphoreType.DMA((16,)),
            pltpu.SemaphoreType.DMA((16,)),
            pltpu.SemaphoreType.DMA((orbs - 1, 4)),
            pltpu.SemaphoreType.DMA((orbs - 1, 4)),
            pltpu.SemaphoreType.DMA((orbs - 1, 4)),
            pltpu.SemaphoreType.DMA((orbs - 1, 4)),
        ],
        compiler_params=pltpu.CompilerParams(vmem_limit_bytes=48 << 20, collective_id=0, has_side_effects=True),
        cost_estimate=pl.CostEstimate(flops=36_000_000_000, bytes_accessed=12 << 20, transcendentals=0),
        name="step",
    )(
        orbitals, near_source.T, far_leaf.T, far_mid.T, far_top, leaf_basis, near_table, transfer,
        coupling, pair_transfer, coarse_coupling,
    )
    return orbitals - RELAX_STEP * change * orbitals


def solution(mesh):
    placed = (P("orb", "space", None),) + (P("space", None),) * 4 + (P(),) * 6
    return jax.shard_map(
        shards, mesh=mesh, in_specs=placed, out_specs=P("orb", "space", None), check_vma=False
    )
```

```python
import jax
import jax.numpy as jnp
from jax import lax
from jax.experimental import pallas as pl
from jax.experimental.pallas import tpu as pltpu
from jax.sharding import PartitionSpec as P

BF = jnp.bfloat16
F32 = jnp.float32
NN = (((1,), (0,)), ((), ()))
NT = (((1,), (1,)), ((), ()))
RELAX_STEP = 0.1
MESH = pl.DeviceIdType.MESH


def dot(a, b, dims=NN):
    return lax.dot_general(a, b, dims, preferred_element_type=F32)


def iota(shape, dim):
    return lax.broadcasted_iota(jnp.int32, shape, dim)


def ones_where(mask):
    return jnp.where(mask, 1.0, 0.0).astype(BF)


def one_hot(places, first, number, rows, width):
    lane = iota((rows, width), 1).astype(BF)
    found = [
        jnp.where(lane == places[:, k : k + 1], BF(1), BF(0)) for k in range(first, first + number)
    ]
    return jnp.concatenate(found, axis=0)


def as_place(numbers):
    return numbers.astype(F32).astype(BF)


def log2(number):
    return number.bit_length() - 1


def octant_picker(parents, half, width):
    row, col = iota((8 * parents, width), 0), iota((8 * parents, width), 1)
    octant, b = row >> log2(parents), row & (parents - 1)
    z, y, x = b >> (2 * log2(half)), (b >> log2(half)) & (half - 1), b & (half - 1)
    dz, dy, dx = octant >> 2, (octant >> 1) & 1, octant & 1
    side = 2 * half
    child = ((2 * z + dz) * side + 2 * y + dy) * side + 2 * x + dx
    return ones_where(child == col)


def merge_up(picked, parents, transfer_ref):
    total = None
    for octant in range(8):
        part = dot(picked[octant * parents : (octant + 1) * parents], transfer_ref[octant])
        total = part if total is None else total + part
    return total.astype(BF)


def spread(matrix):
    zero = jnp.zeros_like(matrix)
    top = jnp.concatenate([matrix, zero], axis=1)
    return jnp.concatenate([top, jnp.concatenate([zero, matrix], axis=1)], axis=0)


def spread_basis(basis_ref, basis2_ref):
    basis2_ref[...] = jnp.zeros((128, 512), BF)
    basis2_ref[0:64, 0:256] = basis_ref[...]
    basis2_ref[64:128, 256:512] = basis_ref[...]


def step_kernel(
    orb_hbm, near_list, leaf_list, mid_list, top_list, basis_ref, table_hbm, transfer_in, coupling_hbm, pair_in, coarse_in,
    out_ref,
    orb_ref, table_ref, coupling_ref, picker_ref, dens_ref, leaf_ref, mid_ref, top_ref, cube_ref, basis2_ref, transfer_ref, pair_ref,
    coarse_ref, weight_ref, near_pick, far_pick, near_ref, near_part, near_other, far_ref, coeff_ref, coeff_part, coeff_other,
    load_sem, halo_send, halo_recv, cube_send, cube_recv, near_send, near_recv, coeff_send, coeff_recv,
):
    me, orb = lax.axis_index("space"), lax.axis_index("orb")
    count, orbs = lax.axis_size("space"), lax.axis_size("orb")
    after, before = lax.rem(me + 1, count), lax.rem(me + count - 1, count)
    barrier = pltpu.get_barrier_semaphore()

    group = min(8, count)
    base = me - lax.rem(me, group)
    mates = [base + lax.rem(me - base + away, group) for away in range(1, group)]
    twins = [lax.rem(me + away, count) for away in range(group, count, group)]
    friends = [(other, orb) for other in mates + twins + [before, after]]
    friends += [(me, lax.rem(orb + away, orbs)) for away in range(1, orbs)]

    def rows_of(c, size):
        return pl.ds(pl.multiple_of(c * size, size), size)

    def load_orbitals(c):
        rows = rows_of(c, 256)
        return pltpu.make_async_copy(orb_hbm.at[:, rows], orb_ref.at[:, rows], load_sem.at[c])

    load_table = pltpu.make_async_copy(table_hbm, table_ref, load_sem.at[4])
    load_coupling = pltpu.make_async_copy(coupling_hbm, coupling_ref, load_sem.at[5])
    for c in range(4):
        load_orbitals(c).start()
    load_table.start()
    load_coupling.start()
    for friend in friends:
        pl.semaphore_signal(barrier, inc=1, device_id=friend, device_id_type=MESH)

    spread_basis(basis_ref, basis2_ref)
    for given, kept in ((pair_in, pair_ref), (coarse_in, coarse_ref), (transfer_in, transfer_ref)):
        for i in range(given.shape[0]):
            kept[i] = spread(given[i])
    picker_ref[...] = octant_picker(32, 4, 256)
    mid_ref[224:256, :] = jnp.zeros((32, 128), BF)
    top_ref[48:128, :] = jnp.zeros((80, 128), BF)

    def moments_chunk(c, _):
        load_orbitals(c).wait()
        rows = rows_of(c, 256)
        inner = pl.ds(pl.multiple_of(64 + c * 256, 64), 256)
        for o in range(2):
            values = orb_ref[o, rows, :]
            dens_ref[inner, o * 256 : (o + 1) * 256] = (values * values).astype(BF)
        leaf = dot(dens_ref[inner, :], basis2_ref[...], NT).astype(BF)
        leaf_ref[pl.ds(pl.multiple_of(192 + c * 256, 64), 256), :] = leaf
        picked = dot(picker_ref[...], leaf).astype(BF)
        mid_ref[pl.ds(pl.multiple_of(48 + c * 32, 16), 32), :] = merge_up(picked, 32, transfer_ref)
        return 0

    lax.fori_loop(0, 4, moments_chunk, 0)

    def halo(number, ref, head, tail, rows, ahead):
        source, target, device = (tail, 0, after) if ahead else (head, tail + rows, before)
        return pltpu.make_async_remote_copy(
            src_ref=ref.at[pl.ds(source, rows)],
            dst_ref=ref.at[pl.ds(target, rows)],
            send_sem=halo_send.at[number],
            recv_sem=halo_recv.at[number],
            device_id=(device, orb),
            device_id_type=MESH,
        )

    halos = []
    for ref, head, tail, rows in (
        (dens_ref, 64, 1024, 64),
        (leaf_ref, 192, 1024, 192),
        (mid_ref, 48, 128, 48),
        (top_ref, 16, 16, 16),
    ):
        for ahead in (False, True):
            halos.append(halo(len(halos), ref, head, tail, rows, ahead))
    top = merge_up(dot(octant_picker(16, 2, 128), mid_ref[48:176, :]).astype(BF), 16, transfer_ref)
    top_ref[16:32, :] = top
    cube_ref[rows_of(me, 16), :] = merge_up(
        dot(octant_picker(16, 1, 16), top).astype(BF), 16, transfer_ref
    )

    def cube_copies(first, blocks, others, stage):
        block = cube_ref.at[pl.ds(pl.multiple_of(first * 16, 16), blocks * 16)]
        return [
            pltpu.make_async_remote_copy(
                src_ref=block,
                dst_ref=block,
                send_sem=cube_send.at[stage + i],
                recv_sem=cube_recv.at[stage + i],
                device_id=(other, orb),
                device_id_type=MESH,
            )
            for i, other in enumerate(others)
        ]

    to_mates = cube_copies(me, 1, mates, 0)
    to_twins = cube_copies(base, group, twins, group - 1)

    def to_orbs(part, landing, send, recv, c, size):
        rows = rows_of(c, size)
        return [
            pltpu.make_async_remote_copy(
                src_ref=part.at[rows],
                dst_ref=landing.at[away - 1, rows],
                send_sem=send.at[away - 1, c],
                recv_sem=recv.at[away - 1, c],
                device_id=(me, lax.rem(orb + away, orbs)),
                device_id_type=MESH,
            )
            for away in range(1, orbs)
        ]

    load_table.wait()
    load_coupling.wait()

    def near_chunk(i, _):
        c = lax.rem(i + 1, 4)

        @pl.when(i == 1)
        def _():
            pl.semaphore_wait(barrier, len(friends))
            for copy in halos + to_mates:
                copy.start()

        @pl.when(i >= 1)
        def _():
            for copy in to_orbs(near_part, near_other, near_send, near_recv, i, 256):
                copy.start()

        @pl.when(i == 2)
        def _():
            for copy in halos[0:2] + to_mates:
                copy.wait()
            for copy in to_twins:
                copy.start()

        for part in range(2):
            base = pl.multiple_of(c * 256 + part * 128, 128)
            place = as_place((near_list[:, pl.ds(base, 128)].T + (64 + 128 * part)) & 255)
            for first in range(0, 27, 3):
                hot = one_hot(place, first, 3, 128, 256)
                for o in range(2):
                    source = dens_ref[pl.ds(base, 256), o * 256 : (o + 1) * 256]
                    at = o * 256 + part * 128
                    picked = dot(hot, source).astype(BF)
                    for k in range(3):
                        near_pick[at : at + 128, (first + k) * 256 : (first + k + 1) * 256] = picked[
                            k * 128 : (k + 1) * 128
                        ]
        total = None
        for k in range(27):
            part = dot(near_pick[:, k * 256 : (k + 1) * 256], table_ref[k], NT)
            total = part if total is None else total + part
        rows = rows_of(c, 256)
        near_ref[rows, 0:256] = total[:256]
        near_ref[rows, 256:512] = total[256:]
        near_part[rows, :] = (total[:256] + total[256:]).astype(BF)
        return 0

    lax.fori_loop(0, 2, near_chunk, 0)
    for k in range(108):
        weight_ref[:, k * 128 : (k + 1) * 128] = spread(coupling_ref[k])

    def pick(place, rows, at, table, beside=iter(())):
        number = 128 // rows
        place = as_place(place)
        for first in range(0, 108, number):
            number = min(number, 108 - first)
            hot = one_hot(place, first, number, rows, table.shape[0])
            picked = dot(hot, table).astype(BF)
            for k in range(number):
                far_pick[at : at + rows, (first + k) * 128 : (first + k + 1) * 128] = picked[
                    k * rows : (k + 1) * rows
                ]
            next(beside, None)

    def far_chunk(c):
        for half in range(2):
            start = pl.multiple_of(c * 256 + half * 128, 128)
            offset = (leaf_list[:, pl.ds(start, 128)].T - start + 192) & 1023
            for layer in range(2):
                base = pl.multiple_of(start + layer * 64, 64)
                table = jnp.concatenate(
                    [leaf_ref[pl.ds(base, 128), :], leaf_ref[pl.ds(base + 320, 128), :]], axis=0
                )
                place = (offset[layer * 64 : (layer + 1) * 64] - 64 * layer) & 1023
                place = jnp.where(place < 128, place, place - 192)
                pick(place, 64, half * 128 + layer * 64, table)
        far_ref[rows_of(c, 256), :] = dot(far_pick[...], weight_ref[...], NT)

    def inner_far(i, _):
        far_chunk(i + 1)
        return 0

    lax.fori_loop(0, 2, inner_far, 0)
    lax.fori_loop(2, 4, near_chunk, 0)
    for copy in to_orbs(near_part, near_other, near_send, near_recv, 0, 256):
        copy.start()

    for copy in halos[2:8]:
        copy.wait()

    for copy in to_twins:
        copy.wait()

    coarse_coeffs = []

    def coarse_tree():
        row, col = iota((64, cube_ref.shape[0]), 0), iota((64, cube_ref.shape[0]), 1)
        cubes = dot(ones_where(col == 16 * (row // 2) + row % 2), cube_ref[...]).astype(BF)
        row, col = iota((64, 64), 0), iota((64, 64), 1)
        child = [ones_where(col == 2 * row + p) for p in range(2)]
        mother = [ones_where((col == row // 2) & (row % 2 == p)) for p in range(2)]
        shift = [
            ones_where((col == row - 3) & (row % 2 == 1)),
            ones_where(col == row - 2),
            ones_where(col == row + 2),
            ones_where((col == row + 3) & (row % 2 == 0)),
        ]
        yield

        def coupled(level, depth):
            total = None
            for w in range(4):
                part = dot(dot(shift[w], level).astype(BF), coarse_ref[w], NT)
                total = part if total is None else total + part
            return total * (0.5 ** (3 + depth))

        level, coupled_levels = cubes, []
        for depth in range(6):
            picked = [dot(child[p], level).astype(BF) for p in range(2)]
            yield
            coupled_levels.append(coupled(level, depth))
            yield
            level = (dot(picked[0], pair_ref[0]) + dot(picked[1], pair_ref[1])).astype(BF)
            yield
        coeffs = coupled(level, 6).astype(BF)
        yield
        for depth in range(5, -1, -1):
            picked = [dot(mother[p], coeffs).astype(BF) for p in range(2)]
            yield
            total = coupled_levels[depth]
            for p in range(2):
                total = total + dot(picked[p], pair_ref[p], NT)
            coeffs = total.astype(BF)
            yield
        coarse_coeffs.append(coeffs)

    steps = coarse_tree()
    mid_place = mid_list[...].T - (me * 128 - 48)
    pick(mid_place[0:64], 64, 0, mid_ref[...], steps)
    pick(mid_place[64:128], 64, 64, mid_ref[...], steps)
    for _ in steps:
        pass
    coeffs = coarse_coeffs[0]
    pick(top_list[...] - (me * 16 - 16), 16, 128, top_ref[...])
    far = dot(far_pick[0:144, :], weight_ref[...], NT)

    def split_down(coeffs, half, first, start, rows):
        parents = coeffs.shape[0]
        side = 2 * half
        row, col = iota((rows, parents), 0) + start, iota((rows, parents), 1)
        z, y, x = row >> (2 * log2(side)), (row >> log2(side)) & (side - 1), row & (side - 1)
        parent = ((z >> 1) * half + (y >> 1)) * half + (x >> 1) + first
        pulled = dot(ones_where(col == parent), coeffs).astype(BF)
        r = iota((rows, 128), 0) + start
        octant = 4 * ((r >> (2 * log2(side))) & 1) + 2 * ((r >> log2(side)) & 1) + (r & 1)
        total = None
        for o in range(8):
            part = dot(jnp.where(octant == o, pulled, jnp.zeros_like(pulled)), transfer_ref[o], NT)
            total = part if total is None else total + part
        return total

    top = 0.25 * far[128:144] + split_down(coeffs, 1, 2 * me, 0, 16)
    mid = 0.5 * far[0:128] + split_down(top.astype(BF), 2, 0, 0, 128)
    mid_ref[0:128, :] = mid.astype(BF)

    def finish_chunk(c):
        leaf = far_ref[rows_of(c, 256), :] + split_down(mid_ref[0:128, :], 4, 0, c * 256, 256)
        leaf = leaf.astype(BF)
        coeff_ref[rows_of(c, 256), :] = leaf
        wide = leaf.astype(F32)
        wide = wide + pltpu.roll(wide, 64, 1)
        packed = jnp.where(iota((128, 128), 1) < 64, wide[0:128], wide[128:256])
        coeff_part[rows_of(c, 128), :] = packed.astype(BF)
        for copy in to_orbs(coeff_part, coeff_other, coeff_send, coeff_recv, c, 128):
            copy.start()

    def finish_inner(i, _):
        finish_chunk(i + 1)
        return 0

    def finish_outer(i, _):
        c = lax.rem(i + 1, 4)
        far_chunk(c)
        finish_chunk(c)
        return 0

    lax.fori_loop(0, 2, finish_inner, 0)
    lax.fori_loop(2, 4, finish_outer, 0)

    def change_chunk(i, _):
        c = lax.rem(i + 1, 4)
        for copy in to_orbs(near_part, near_other, near_send, near_recv, c, 256):
            copy.wait()
        for copy in to_orbs(coeff_part, coeff_other, coeff_send, coeff_recv, c, 128):
            copy.wait()
        rows, packed_rows = rows_of(c, 256), rows_of(c, 128)
        packed = coeff_part[packed_rows, :].astype(F32)
        hartree = near_part[rows, :].astype(F32)
        for away in range(orbs - 1):
            packed = packed + coeff_other[away, packed_rows, :].astype(F32)
            hartree = hartree + near_other[away, rows, :].astype(F32)
        both = dot(packed.astype(BF), basis2_ref[...])
        hartree = hartree + jnp.concatenate([both[:, :256], both[:, 256:]], axis=0)
        potential = near_ref[rows, :] + dot(coeff_ref[rows, :], basis2_ref[...])
        for o in range(2):
            out_ref[o, rows, :] = hartree - potential[:, o * 256 : (o + 1) * 256]
        return 0

    lax.fori_loop(0, 4, change_chunk, 0)


def shards(
    orbitals, near_source, far_leaf, far_mid, far_top, leaf_basis, near_table, transfer, coupling, pair_transfer,
    coarse_coupling,
):
    count, orbs = lax.axis_size("space"), lax.axis_size("orb")
    near_by, here = pl.BlockSpec(memory_space=pl.ANY), pl.BlockSpec(memory_space=pltpu.VMEM)
    change = pl.pallas_call(
        step_kernel,
        in_specs=[near_by, here, here, here, here, here, near_by, here, near_by, here, here],
        out_specs=here,
        out_shape=jax.ShapeDtypeStruct((2, 1024, 256), F32),
        scratch_shapes=[
            pltpu.VMEM((2, 1024, 256), F32),
            pltpu.VMEM((27, 256, 256), BF),
            pltpu.VMEM((108, 64, 64), BF),
            pltpu.VMEM((256, 256), BF),
            pltpu.VMEM((1152, 512), BF),
            pltpu.VMEM((1408, 128), BF),
            pltpu.VMEM((256, 128), BF),
            pltpu.VMEM((128, 128), BF),
            pltpu.VMEM((count * 16, 128), BF),
            pltpu.VMEM((128, 512), BF),
            pltpu.VMEM((8, 128, 128), BF),
            pltpu.VMEM((2, 128, 128), BF),
            pltpu.VMEM((4, 128, 128), BF),
            pltpu.VMEM((128, 108 * 128), BF),
            pltpu.VMEM((512, 27 * 256), BF),
            pltpu.VMEM((256, 108 * 128), BF),
            pltpu.VMEM((1024, 512), F32),
            pltpu.VMEM((1024, 256), BF),
            pltpu.VMEM((orbs - 1, 1024, 256), BF),
            pltpu.VMEM((1024, 128), F32),
            pltpu.VMEM((1024, 128), BF),
            pltpu.VMEM((512, 128), BF),
            pltpu.VMEM((orbs - 1, 512, 128), BF),
            pltpu.SemaphoreType.DMA((6,)),
            pltpu.SemaphoreType.DMA((8,)),
            pltpu.SemaphoreType.DMA((8,)),
            pltpu.SemaphoreType.DMA((16,)),
            pltpu.SemaphoreType.DMA((16,)),
            pltpu.SemaphoreType.DMA((orbs - 1, 4)),
            pltpu.SemaphoreType.DMA((orbs - 1, 4)),
            pltpu.SemaphoreType.DMA((orbs - 1, 4)),
            pltpu.SemaphoreType.DMA((orbs - 1, 4)),
        ],
        compiler_params=pltpu.CompilerParams(vmem_limit_bytes=48 << 20, collective_id=0, has_side_effects=True),
        cost_estimate=pl.CostEstimate(flops=36_000_000_000, bytes_accessed=12 << 20, transcendentals=0),
        name="step",
    )(
        orbitals, near_source.T, far_leaf.T, far_mid.T, far_top, leaf_basis, near_table, transfer,
        coupling, pair_transfer, coarse_coupling,
    )
    return orbitals - RELAX_STEP * change * orbitals


def solution(mesh):
    placed = (P("orb", "space", None),) + (P("space", None),) * 4 + (P(),) * 6
    return jax.shard_map(
        shards, mesh=mesh, in_specs=placed, out_specs=P("orb", "space", None), check_vma=False
    )
```
